128 devices in a mesh: round: 2 (over core), head: 2 (over x_hi), seq: 32 (over y, x_lo, z).
Axes of the slice: x: 4 (x_hi: 2, x_lo: 2; x = x_hi * 2 + x_lo), y: 4, z: 4, core: 2. Of those that a mesh axis runs over, the one named last changes fastest.
Arguments:
- tokens: bfloat16 [32768, 1024], P(('round', 'head', 'seq')), may hold values from -48 to 48
- w_qk: bfloat16 [1024, 1024], replicated, may hold values from -0.375 to 0.375
- w_v: bfloat16 [1024, 1024], replicated, may hold values from -0.1875 to 0.1875
- w_out: bfloat16 [1024, 1024], replicated, may hold values from -0.375 to 0.375
- positions: int32 [2, 32768], P(None, ('round', 'head', 'seq')), may hold values from 0 to 32767, as said below
- buckets: int32 [2, 32768], P('round', 'seq'), may hold values from 0 to 1022, as said below
Outputs:
- layer_out: bfloat16 [32768, 1024], P(('round', 'head', 'seq'))
The draws below stay inside these ranges and needn't reach their ends.
Inputs may be any that keep to these rules, and one draw needn't show every extreme that they name: Each row is a permutation: every sorted position appears once. Of the 256 tokens of one device, at most 14 have positions of one round in one range of 1024 sorted positions starting at a multiple of 1024. `buckets`: along each row the bucket numbers never fall, except that the last run of positions carries bucket 0 again: the bucket of the first positions continues around the end of the row.
All inputs are finite; a program needn't handle non-finite values.
Results may differ from the reference program's by a relative error of at most 0.022.
Values may be sent and summed in bfloat16 or wider, within the bound.
No kernel may reach another device: no remote copies, remote signals or barrier semaphores. Data moves between devices by JAX's collectives and lax.ppermute only.
A program may use at most 64 MiB of HBM per device.

```python
import jax
import jax.numpy as jnp
from jax import lax

D = 1024
H = 8
DH = 128
R = 2
BLOCK = 1024
TOK_DEV = 256
TOKENS = 32768
NBLOCKS = 32
NBUCKETS = 1024
N_SEQ = 32


def route_plan(key):
    sources = TOKENS // TOK_DEV
    share_len = TOK_DEV // N_SEQ
    half_len = share_len // 2
    quarter_len = share_len // 4
    placings = []
    for round_index in range(R):
        round_key = jax.random.fold_in(key, 100 + round_index)
        key_one, key_two, key_three, key_four = jax.random.split(round_key, 4)
        lead_order = jax.random.permutation(key_one, N_SEQ).astype(jnp.int32)
        tail_order = 1 + jax.random.permutation(key_two, N_SEQ - 1).astype(jnp.int32)
        pair_order = lead_order[jnp.concatenate([jnp.zeros((1,), jnp.int32), tail_order])]
        sources_at = jnp.arange(sources, dtype=jnp.int32) % N_SEQ
        next_owner = (sources_at + 1) % N_SEQ
        columns = jnp.arange(N_SEQ, dtype=jnp.int32)[None, :]
        lead_gain = (columns == lead_order[sources_at][:, None]).astype(jnp.int32) - (columns == lead_order[next_owner][:, None]).astype(jnp.int32)
        pair_gain = (columns == pair_order[sources_at][:, None]).astype(jnp.int32) - (columns == pair_order[next_owner][:, None]).astype(jnp.int32)
        counts = share_len + half_len * lead_gain + quarter_len * pair_gain
        bounds = jnp.cumsum(counts, axis=1)
        jitter = jax.random.randint(key_three, (sources, TOK_DEV), 0, 2 ** 18).astype(jnp.int32)
        sort_key = jitter * TOK_DEV + jnp.arange(TOK_DEV, dtype=jnp.int32)[None, :]
        ranking = jnp.argsort(jnp.argsort(sort_key, axis=1), axis=1).astype(jnp.int32)
        owner_of = jnp.sum((ranking[:, :, None] >= bounds[:, None, :]).astype(jnp.int32), axis=2)
        shuffle = jax.random.permutation(key_four, TOKENS).astype(jnp.int32)
        token_order = jnp.argsort(owner_of.reshape(-1) * TOKENS + shuffle).astype(jnp.int32)
        placing = jnp.zeros((TOKENS,), jnp.int32).at[token_order].set(jnp.arange(TOKENS, dtype=jnp.int32))
        placings.append(placing)
    return jnp.stack(placings)


def bucket_plan(key):
    margin = BLOCK // 4
    labels = []
    for round_index in range(R):
        round_key = jax.random.fold_in(key, 200 + round_index)
        cut_at = jax.random.permutation(round_key, TOKENS - 2 * margin).astype(jnp.int32)[:NBUCKETS - 1] + margin
        marker = jnp.zeros((TOKENS,), jnp.int32).at[cut_at].set(1)
        counted = jnp.cumsum(marker).astype(jnp.int32)
        labels.append(jnp.where(counted == NBUCKETS - 1, 0, counted).astype(jnp.int32))
    return jnp.stack(labels)


def draw_positions(key, part):
    shared_plan = route_plan(key)
    return shared_plan


def draw_buckets(key, part):
    shared_labels = bucket_plan(key)
    return shared_labels


def draw_tokens(key, part):
    key = jax.random.fold_in(key, 3)
    key_two = jax.random.fold_in(key, 1)
    base_rows = jnp.clip(jax.random.normal(key_two, (TOKENS, D), jnp.float32), -6.0, 6.0)
    return base_rows.astype(jnp.bfloat16)


def centred(rng, dims, scale, bound, held_as=jnp.bfloat16):
    return jnp.clip(scale * jax.random.normal(rng, dims, jnp.float32), -bound, bound).astype(held_as)


def setup_inputs(seed: int = 0) -> dict:
    splits = jax.random.split(jax.random.key(seed), 7)
    return {
        "tokens": draw_tokens(jax.random.fold_in(splits[6], 71), 0),
        "w_qk": centred(splits[1], (D, H * DH), (D // 4) ** -0.5, 0.375),
        "w_v": centred(splits[2], (D, H * DH), D ** -0.5, 0.1875),
        "w_out": centred(splits[3], (H * DH, D), (H * DH // 4) ** -0.5, 0.375),
        "positions": draw_positions(jax.random.fold_in(splits[6], 71), 0),
        "buckets": draw_buckets(jax.random.fold_in(splits[6], 71), 0),
    }


SELF_PENALTY = -100000.0
BUCKET_PENALTY = -1000000000.0
EPSILON = 1e-06

def key_scaling(rows):
    feature_len = rows.shape[-1]
    squares = lax.optimization_barrier(jnp.mean(jnp.square(rows.astype(jnp.float32)), axis=-1))
    return lax.rsqrt(squares + EPSILON) * feature_len ** (-0.5)

def attend(queries, key_rows, values, scaling, query_bucket, key_bucket):
    block_len = queries.shape[0]
    products = lax.dot_general(queries, key_rows, (((1,), (1,)), ((), ())), preferred_element_type=jnp.float32)
    scores = products * scaling[None, :]
    row_index = jnp.arange(block_len, dtype=jnp.int32)[:, None]
    col_index = jnp.arange(2 * block_len, dtype=jnp.int32)[None, :]
    matching = query_bucket[:, None] == key_bucket[None, :]
    scores = jnp.where(col_index == row_index + block_len, SELF_PENALTY, jnp.where(matching, scores, BUCKET_PENALTY))
    maximum = lax.optimization_barrier(jnp.max(scores, axis=1, keepdims=True))
    powers = jnp.exp(scores - maximum)
    totals = lax.optimization_barrier(jnp.sum(powers, axis=1, keepdims=True))
    weights = (powers / totals).astype(jnp.bfloat16)
    result = jnp.dot(weights, values, preferred_element_type=jnp.float32).astype(jnp.bfloat16)
    return (result, maximum[:, 0] + jnp.log(totals[:, 0]))

def reference(tokens, w_qk, w_v, w_out, positions, buckets):
    query_keys = jnp.dot(tokens, w_qk, preferred_element_type=jnp.float32).astype(jnp.bfloat16).reshape(TOKENS, H, DH)
    values_all = jnp.dot(tokens, w_v, preferred_element_type=jnp.float32).astype(jnp.bfloat16).reshape(TOKENS, H, DH)
    round_results = []
    round_sums = []
    for round_index in range(R):
        sorted_tokens = jnp.argsort(positions[round_index]).astype(jnp.int32)
        bucket_row = buckets[round_index]
        head_results = []
        head_sums = []
        for head_index in range(H):
            sorted_keys = query_keys[sorted_tokens, head_index]
            sorted_values = values_all[sorted_tokens, head_index]
            scaling = key_scaling(sorted_keys)

            def block_step(block_index):
                begin_at = block_index * BLOCK
                prior_at = (block_index + NBLOCKS - 1) % NBLOCKS * BLOCK

                def window(array):
                    return jnp.concatenate([lax.dynamic_slice_in_dim(array, prior_at, BLOCK, 0), lax.dynamic_slice_in_dim(array, begin_at, BLOCK, 0)], axis=0)
                return attend(lax.dynamic_slice_in_dim(sorted_keys, begin_at, BLOCK, 0), window(sorted_keys), window(sorted_values), window(scaling), lax.dynamic_slice_in_dim(bucket_row, begin_at, BLOCK, 0), window(bucket_row))
            results, sums = lax.map(block_step, jnp.arange(NBLOCKS, dtype=jnp.int32))
            placing = positions[round_index]
            head_results.append(results.reshape(TOKENS, DH)[placing])
            head_sums.append(sums.reshape(TOKENS)[placing])
        round_results.append(jnp.stack(head_results))
        round_sums.append(jnp.stack(head_sums))
    per_round = jnp.stack(round_results)
    per_sum = jnp.stack(round_sums)
    largest = lax.optimization_barrier(jnp.max(per_sum, axis=0, keepdims=True))
    shares = jnp.exp(per_sum - largest)
    combined = (lax.optimization_barrier(jnp.sum(shares[..., None] * per_round.astype(jnp.float32), axis=0)) / lax.optimization_barrier(jnp.sum(shares, axis=0))[..., None]).astype(jnp.bfloat16)
    side_by_side = jnp.transpose(combined, (1, 0, 2)).reshape(TOKENS, H * DH)
    return jnp.dot(side_by_side, w_out, preferred_element_type=jnp.float32).astype(jnp.bfloat16)
```

```python
import functools

import jax
import jax.numpy as jnp
from jax import lax
from jax.experimental import pallas as pl
from jax.experimental.pallas import tpu as pltpu
from jax.sharding import PartitionSpec as P

DH = 128
BLOCK = 1024
TILE = 128
SLOTS = 16
META = 14
SHIFT = 1024

SELF_PENALTY = -100000.0
BUCKET_PENALTY = -1000000000.0
EPSILON = 1e-06
LOWEST = -3.0e38

BF = jnp.bfloat16
F32 = jnp.float32
I32 = jnp.int32
NT = (((1,), (1,)), ((), ()))


def iota(shape, dim):
    return lax.broadcasted_iota(I32, shape, dim)


def mask(cond):
    return jnp.where(cond, 1.0, 0.0).astype(BF)


def mm(a, b):
    return jnp.dot(a, b, preferred_element_type=F32)


def mm_nt(a, b):
    return lax.dot_general(a, b, NT, preferred_element_type=F32)


def full(shape):
    return pl.BlockSpec(shape, lambda *_: (0,) * len(shape))


def slots_of(pos, owners):
    count = pos.shape[1]
    dest = pos >> 10
    hot = iota((owners, count), 0) == dest
    earlier = mask(iota((count, count), 0) < iota((count, count), 1))
    before = mm(mask(hot), earlier)
    rank = jnp.sum(jnp.where(hot, before, 0.0), axis=0, keepdims=True).astype(I32)
    return dest, hot, rank


def pack_kernel(tok_ref, pos_ref, out_ref, *, owners):
    count = tok_ref.shape[0]
    width = out_ref.shape[1]
    rows = owners * SLOTS
    tokens = tok_ref[...]
    for r in range(2):
        pos = pos_ref[r : r + 1, :]
        dest, hot, rank = slots_of(pos, owners)
        within = pos & (BLOCK - 1)
        slot = dest * SLOTS + rank
        body = mm(mask(iota((rows, count), 0) == slot), tokens)
        value = iota((128, count), 0)
        code = jnp.where((value & 1) == 0, (within >> 5) + 1, within & 31)
        code = jnp.where((value >> 1) == rank, code, 0).astype(F32).astype(BF)
        places = mm_nt(mask(hot), code).astype(BF)
        at_meta = mask(iota((rows, owners), 0) == iota((rows, owners), 1) * SLOTS + META)
        extra = mm(at_meta, places)
        for a in range(2):
            at = (a * 2 + r) * rows
            out_ref[at : at + rows, 0:128] = (
                body[:, a * width : a * width + 128] + extra
            ).astype(BF)
            out_ref[at : at + rows, 128:width] = body[
                :, a * width + 128 : (a + 1) * width
            ].astype(BF)


def meta_of(x_ref):
    rows = x_ref.shape[0]
    count = rows // SLOTS
    pick = mask(iota((count, rows), 1) == iota((count, rows), 0) * SLOTS + META)
    return mm(pick, x_ref[:, 0:128]).astype(BF)


def place_rows(meta):
    count = meta.shape[0]
    v, lane = iota((128, 128), 0), iota((128, 128), 1)
    j = lane & (SLOTS - 1)
    weight = jnp.where(v == 2 * j, 32.0, jnp.where(v == 2 * j + 1, 1.0, 0.0)).astype(BF)
    codes = mm(meta, weight)
    own = (iota((count, 128), 0) & 7) == (iota((count, 128), 1) >> 4)
    codes = jnp.where(own, codes, 0.0)
    return jnp.sum(codes.reshape(count // 8, 8, 128), axis=1)


def place_columns(meta, first, rows):
    count = meta.shape[0]
    slot = iota((rows, count), 0) + first
    source = mask((slot >> 4) == iota((rows, count), 1))
    values = mm(source, meta)
    lane = iota((rows, 128), 1)
    keep = (lane >> 1) == (iota((rows, 128), 0) & (SLOTS - 1))
    values = jnp.where(keep, values, 0.0).astype(BF)
    weight = jnp.where((iota((128, 128), 0) & 1) == 0, 32.0, 1.0).astype(BF)
    return mm(values, weight)


def sort_kernel(x_ref, low_ref, high_ref, meta_ref, code_ref):
    meta = meta_of(x_ref)
    meta_ref[...] = meta
    codes = place_rows(meta)
    code_ref[...] = codes
    chunks = codes.shape[0]
    half = low_ref.shape[0]
    step = 256

    def rows_at(start, out_ref, at):
        position = (iota((step, 128), 0) + start + 32).astype(F32)
        picks = [
            mask(position == jnp.broadcast_to(code_ref[q : q + 1, :], (step, 128)))
            for q in range(chunks)
        ]
        out_ref[pl.ds(at, step), :] = mm(jnp.concatenate(picks, axis=1), x_ref[...]).astype(BF)

    for t in range(half // step):
        rows_at(half + t * step, high_ref, t * step)
    for t in range(half // step):
        rows_at(t * step, low_ref, t * step)


def project(mine, other, wm, wo):
    return (mm(mine, wm) + mm(other, wo)).astype(BF)


def key_scales(keys):
    sq = jnp.square(keys.astype(F32))
    top = sq.astype(BF)
    rest = (sq - top.astype(F32)).astype(BF)
    ones = jnp.ones((8, DH), BF)
    total = mm_nt(ones, top) + mm_nt(ones, rest)
    return lax.rsqrt(total * (1.0 / DH) + EPSILON) * DH ** (-0.5)


def lse_lanes(tile, lse, head):
    top = lse.astype(BF).astype(F32)
    rest = lse - top
    lane = iota(tile.shape, 1) & 7
    return jnp.where(lane == 2 * head, top, jnp.where(lane == 2 * head + 1, rest, tile))


def masked(products, scale, query_label, key_label, self_at):
    cols = products.shape[1]
    match = jnp.concatenate(
        [query_label == key_label[:, c : c + TILE] for c in range(0, cols, TILE)], axis=1
    )
    scores = jnp.where(match, products * scale, BUCKET_PENALTY)
    diagonal = iota(products.shape, 1) - iota(products.shape, 0) == self_at
    return jnp.where(diagonal, SELF_PENALTY, scores)


def own_kernel(
    info_ref, lm_ref, hm_ref, lo_ref, ho_ref, wqm_ref, wqo_ref, wvm_ref, wvo_ref,
    row_ref, col_ref, q_ref, v_ref, scale_ref, out_ref, lse_ref,
):
    half = lm_ref.shape[0]
    heads = q_ref.shape[1] // DH
    for m_ref, o_ref, at in ((hm_ref, ho_ref, half), (lm_ref, lo_ref, 0)):
        mine, other = m_ref[...], o_ref[...]
        q_ref[at : at + half, :] = project(mine, other, wqm_ref[...], wqo_ref[...])
        v_ref[at : at + half, :] = project(mine, other, wvm_ref[...], wvo_ref[...])
    for h in range(heads):
        scale_ref[h * 8 : h * 8 + 8, :] = key_scales(q_ref[:, h * DH : (h + 1) * DH])
    tiles = BLOCK // TILE
    band = 3 * TILE

    @pl.loop(0, tiles)
    def _(i):
        at = pl.multiple_of(i * TILE, TILE)
        start = pl.multiple_of(jnp.clip(i - 1, 0, tiles - 3) * TILE, TILE)

        @pl.when(info_ref[2 + i] == 0)
        def _():
            query_label = col_ref[pl.ds(at, TILE), :]
            key_label = row_ref[0:1, pl.ds(start, band)]
            lse_tile = jnp.zeros((TILE, 128), F32)
            for h in range(heads):
                cols = slice(h * DH, (h + 1) * DH)
                products = mm_nt(q_ref[pl.ds(at, TILE), cols], q_ref[pl.ds(start, band), cols])
                scale = scale_ref[h * 8 : h * 8 + 1, pl.ds(start, band)]
                scores = masked(products, scale, query_label, key_label, at - start)
                top = jnp.max(scores, axis=1, keepdims=True)
                powers = jnp.exp(scores - top)
                total = jnp.sum(powers, axis=1, keepdims=True)
                result = mm(powers.astype(BF), v_ref[pl.ds(start, band), cols])
                out_ref[pl.ds(at, TILE), cols] = (result / total).astype(BF)
                lse_tile = lse_lanes(lse_tile, top + jnp.log(total), h)
            lse_ref[pl.ds(at, TILE), :] = lse_tile.astype(BF)

        @pl.when(info_ref[2 + i] != 0)
        def _():
            out_ref[pl.ds(at, TILE), :] = jnp.zeros((TILE, heads * DH), BF)
            lse_ref[pl.ds(at, TILE), :] = jnp.zeros((TILE, 128), BF)


def rest_kernel(
    info_ref, xm_ref, xo_ref, wqm_ref, wqo_ref, wvm_ref, wvo_ref, row_ref, col_ref,
    q_ref, v_ref, scale_ref, own_ref, own_lse_ref, meta_ref, send_ref,
    out_ref, lse_ref, pk_ref, pv_ref, ps_ref, m_ref, l_ref, acc_ref,
):
    halo = xm_ref.shape[0]
    heads = q_ref.shape[1] // DH
    tiles = BLOCK // TILE
    skipped = (BLOCK - halo) // TILE
    flags = 2 + tiles
    used = flags + tiles * 2 * tiles
    out_ref[...] = own_ref[...]
    lse_ref[...] = own_lse_ref[...]

    @pl.loop(0, halo // TILE)
    def _(t):
        @pl.when(info_ref[used + skipped + t] != 0)
        def _():
            at = pl.multiple_of(t * TILE, TILE)
            mine, other = xm_ref[pl.ds(at, TILE), :], xo_ref[pl.ds(at, TILE), :]
            keys = project(mine, other, wqm_ref[...], wqo_ref[...])
            pk_ref[pl.ds(at, TILE), :] = keys
            pv_ref[pl.ds(at, TILE), :] = project(mine, other, wvm_ref[...], wvo_ref[...])
            for h in range(heads):
                ps_ref[h * 8 : h * 8 + 8, pl.ds(at, TILE)] = key_scales(
                    keys[:, h * DH : (h + 1) * DH]
                )

    @pl.loop(0, tiles)
    def _(i):
        @pl.when(info_ref[2 + i] != 0)
        def _():
            at = pl.multiple_of(i * TILE, TILE)
            query_label = col_ref[pl.ds(at, TILE), :]
            m_ref[...] = jnp.full(m_ref.shape, LOWEST, F32)
            l_ref[...] = jnp.zeros(l_ref.shape, F32)
            acc_ref[...] = jnp.zeros(acc_ref.shape, F32)

            def add(keys_ref, values_ref, scales_ref, key_at, label_at, self_at):
                key_label = row_ref[0:1, pl.ds(label_at, TILE)]
                for h in range(heads):
                    cols = slice(h * DH, (h + 1) * DH)
                    products = mm_nt(
                        q_ref[pl.ds(at, TILE), cols], keys_ref[pl.ds(key_at, TILE), cols]
                    )
                    scale = scales_ref[h * 8 : h * 8 + 1, pl.ds(key_at, TILE)]
                    scores = masked(products, scale, query_label, key_label, self_at)
                    old = m_ref[:, cols]
                    top = jnp.maximum(old, jnp.max(scores, axis=1, keepdims=True))
                    powers = jnp.exp(scores - top)
                    shrink = jnp.exp(old - top)
                    m_ref[:, cols] = top
                    l_ref[:, cols] = l_ref[:, cols] * shrink + jnp.sum(
                        powers, axis=1, keepdims=True
                    )
                    acc_ref[:, cols] = acc_ref[:, cols] * shrink + mm(
                        powers.astype(BF), values_ref[pl.ds(key_at, TILE), cols]
                    )

            @pl.loop(0, halo // TILE)
            def _(t):
                @pl.when(info_ref[flags + i * 2 * tiles + skipped + t] != 0)
                def _():
                    add(
                        pk_ref, pv_ref, ps_ref, pl.multiple_of(t * TILE, TILE),
                        pl.multiple_of((skipped + t) * TILE, TILE), -4 * BLOCK,
                    )

            @pl.loop(0, tiles)
            def _(t):
                @pl.when(info_ref[flags + i * 2 * tiles + tiles + t] != 0)
                def _():
                    key_at = pl.multiple_of(t * TILE, TILE)
                    add(
                        q_ref, v_ref, scale_ref, key_at,
                        pl.multiple_of(BLOCK + t * TILE, TILE), at - key_at,
                    )

            lse_tile = jnp.zeros((TILE, 128), F32)
            for h in range(heads):
                cols = slice(h * DH, (h + 1) * DH)
                total = l_ref[:, cols]
                out_ref[pl.ds(at, TILE), cols] = (acc_ref[:, cols] / total).astype(BF)
                lse_tile = lse_lanes(lse_tile, m_ref[:, cols] + jnp.log(total), h)
            lse_ref[pl.ds(at, TILE), :] = lse_tile.astype(BF)

    step = 256

    @pl.loop(0, send_ref.shape[0] // step)
    def _(t):
        at = pl.multiple_of(t * step, step)
        codes = place_columns(meta_ref[...], at, step)
        lane = (iota((step, 128), 1) + 32).astype(F32)
        pick = jnp.concatenate(
            [mask(codes == lane + float(c)) for c in range(0, BLOCK, 128)], axis=1
        )
        body = mm(pick, out_ref[...])
        sums = mm(pick, lse_ref[...])
        row = iota((step, 128), 0) & (SLOTS - 1)
        sums = jnp.where(row == (iota((step, 128), 1) >> 3), sums, 0.0)
        sums = jnp.sum(sums.reshape(step // SLOTS, SLOTS, 128), axis=1, keepdims=True)
        sums = jnp.broadcast_to(sums, (step // SLOTS, SLOTS, 128)).reshape(step, 128)
        extra = jnp.where(row == META, sums, 0.0)
        send_ref[pl.ds(at, step), 0:128] = (body[:, 0:128] + extra).astype(BF)
        send_ref[pl.ds(at, step), 128:] = body[:, 128:].astype(BF)


def final_kernel(x_ref, pos_ref, w_ref, out_ref, *, owners):
    count = out_ref.shape[0]
    width = x_ref.shape[1]
    rows = owners * SLOTS
    heads = width // DH
    lane = iota((count, 128), 1)
    picks, meta_picks, ranks = [], [], []
    for r in range(2):
        dest, _, rank = slots_of(pos_ref[r : r + 1, :], owners)
        slot = (dest * SLOTS + rank).astype(F32)
        slot = jnp.transpose(jnp.broadcast_to(slot, (128, count))).astype(I32)
        place = slot & (SLOTS - 1)
        at_meta = slot - place + META
        picks.append(
            jnp.concatenate([mask(slot == lane + c) for c in range(0, rows, 128)], axis=1)
        )
        meta_picks.append(
            jnp.concatenate([mask(at_meta == lane + c) for c in range(0, rows, 128)], axis=1)
        )
        ranks.append(place)
    v = iota((128, width), 0) & 7
    select = mask((v >> 1) == (iota((128, width), 1) >> 7))
    total = None
    for a in range(2):
        values, sums = [], []
        for r in range(2):
            at = (a * 2 + r) * rows
            values.append(mm(picks[r], x_ref[at : at + rows, :]))
            own = mm(meta_picks[r], x_ref[at : at + rows, 0:128])
            own = jnp.where((lane >> 3) == ranks[r], own, 0.0).astype(BF)
            sums.append(mm(own, select))
        largest = jnp.maximum(sums[0], sums[1])
        first, second = jnp.exp(sums[0] - largest), jnp.exp(sums[1] - largest)
        combined = ((first * values[0] + second * values[1]) / (first + second)).astype(BF)
        part = mm(combined, w_ref[a * width : (a + 1) * width, :])
        total = part if total is None else total + part
    out_ref[...] = total.astype(BF)


def window_plan(own, prior):
    first = prior[0]
    own = jnp.where(own < first, own + SHIFT, own).reshape(-1, TILE)
    prior = jnp.where(prior < first, prior + SHIFT, prior).reshape(-1, TILE)
    keys = jnp.concatenate([prior, own], axis=0)
    low, high = jnp.min(keys, axis=1), jnp.max(keys, axis=1)
    tiles = own.shape[0]
    own_low, own_high = low[tiles:], high[tiles:]
    meets = (low[None, :] <= own_high[:, None]) & (high[None, :] >= own_low[:, None])
    tile = jnp.arange(tiles, dtype=I32)[:, None]
    key = jnp.arange(-tiles, tiles, dtype=I32)[None, :]
    start = jnp.clip(tile - 1, 0, tiles - 3)
    outside = jnp.any(meets & ((key < start) | (key > start + 2)), axis=1)
    return outside, meets


def shards(tokens, w_qk, w_v, w_out, positions, buckets):
    tok_dev, model_width = tokens.shape
    owners = lax.axis_size("seq")
    everyone = ("round", "head", "seq")
    total = 2 * 2 * owners
    width = model_width // 2
    heads = width // DH
    rows = total * SLOTS
    half = BLOCK // 2
    tiles = BLOCK // TILE
    core = lax.axis_index("round")
    my_round = lax.axis_index("head")
    block = lax.axis_index("seq")
    call = functools.partial(pl.pallas_call)
    params = pltpu.CompilerParams(vmem_limit_bytes=48 * 1024 * 1024)

    def shape(*dims, dtype=BF):
        return jax.ShapeDtypeStruct(dims, dtype)

    def swap(x):
        return lax.ppermute(x, "round", [(0, 1), (1, 0)])

    def onward(x):
        return lax.ppermute(x, "seq", [(i, (i + 1) % owners) for i in range(owners)])

    def exchange(x):
        x = x.reshape(total, SLOTS, width)
        x = lax.all_to_all(x, everyone, split_axis=0, concat_axis=0, tiled=True)
        return x.reshape(rows, width)

    packed = call(
        functools.partial(pack_kernel, owners=owners),
        out_shape=shape(rows, width),
        compiler_params=params,
        name="pack",
    )(tokens, positions)
    labels = lax.all_gather(buckets[0], ("round", "seq")).reshape(2, owners, BLOCK)
    arrived = exchange(packed)

    low, high, meta, _ = call(
        sort_kernel,
        out_shape=[
            shape(half, width),
            shape(half, width),
            shape(total, 128),
            shape(total // 8, 128, dtype=F32),
        ],
        compiler_params=params,
        name="sort_rows",
    )(arrived)
    halo_high = onward(high)
    low_other, high_other = swap(low), swap(high)

    before = jnp.roll(labels, 1, axis=1)
    first = before[:, :, :1]
    moved = jnp.where(labels < first, labels + SHIFT, labels)
    moved_before = jnp.where(before < first, before + SHIFT, before)
    wide = jnp.any(
        jnp.max(moved_before[:, :, :half], axis=2) >= jnp.min(moved, axis=2)
    )
    own_label = labels[my_round, block]
    prior_label = before[my_round, block]
    outside, meets = window_plan(own_label, prior_label)
    needed = jnp.any(meets[:, :tiles] & outside[:, None], axis=0)
    info = jnp.concatenate(
        [
            jnp.stack([core, 1 - core]).astype(I32),
            outside.astype(I32),
            meets.astype(I32).reshape(-1),
            needed.astype(I32),
        ]
    )
    label_row = jnp.concatenate([prior_label, own_label])[None, :]
    label_col = jnp.broadcast_to(own_label[:, None], (BLOCK, TILE))

    def weight(flip):
        return pl.BlockSpec((width, width), lambda i, s: (s[flip], s[0]))

    weights = [weight(0), weight(1), weight(0), weight(1)]
    weight_args = (w_qk, w_qk, w_v, w_v)
    halves = full((half, width))
    wide_rows = full((BLOCK, width))
    queries, values, scales, own_out, own_lse = call(
        own_kernel,
        out_shape=[
            shape(BLOCK, width),
            shape(BLOCK, width),
            shape(heads * 8, BLOCK, dtype=F32),
            shape(BLOCK, width),
            shape(BLOCK, 128),
        ],
        grid_spec=pltpu.PrefetchScalarGridSpec(
            num_scalar_prefetch=1,
            grid=(1,),
            in_specs=[halves] * 4 + weights + [full((1, BLOCK)), full((BLOCK, TILE))],
            out_specs=[
                wide_rows,
                wide_rows,
                full((heads * 8, BLOCK)),
                wide_rows,
                full((BLOCK, 128)),
            ],
        ),
        compiler_params=params,
        name="own_block",
    )(info, low, high, low_other, high_other, *weight_args, label_row[:, BLOCK:], label_col)

    def finish(halo_mine, halo_other):
        halo = halo_mine.shape[0]
        return call(
            rest_kernel,
            out_shape=shape(rows, width),
            grid_spec=pltpu.PrefetchScalarGridSpec(
                num_scalar_prefetch=1,
                grid=(1,),
                in_specs=[full((halo, width))] * 2
                + weights
                + [
                    full((1, 2 * BLOCK)),
                    full((BLOCK, TILE)),
                    wide_rows,
                    wide_rows,
                    full((heads * 8, BLOCK)),
                    wide_rows,
                    full((BLOCK, 128)),
                    full((total, 128)),
                ],
                out_specs=full((rows, width)),
                scratch_shapes=[
                    pltpu.VMEM((BLOCK, width), BF),
                    pltpu.VMEM((BLOCK, 128), BF),
                    pltpu.VMEM((halo, width), BF),
                    pltpu.VMEM((halo, width), BF),
                    pltpu.VMEM((heads * 8, halo), F32),
                    pltpu.VMEM((TILE, width), F32),
                    pltpu.VMEM((TILE, width), F32),
                    pltpu.VMEM((TILE, width), F32),
                ],
            ),
            compiler_params=params,
            name="prior_block",
        )(
            info, halo_mine, halo_other, *weight_args, label_row, label_col,
            queries, values, scales, own_out, own_lse, meta,
        )

    halo_high_other = swap(halo_high)

    def whole_window():
        halo_low = onward(low)
        return finish(
            jnp.concatenate([halo_low, halo_high], axis=0),
            jnp.concatenate([swap(halo_low), halo_high_other], axis=0),
        )

    back = lax.cond(wide, whole_window, lambda: finish(halo_high, halo_high_other))
    returned = exchange(back)
    return call(
        functools.partial(final_kernel, owners=owners),
        out_shape=shape(tok_dev, model_width),
        compiler_params=params,
        name="combine",
    )(returned, positions, w_out)


def solution(mesh):
    in_specs = (
        P(("round", "head", "seq"), None),
        P(),
        P(),
        P(),
        P(None, ("round", "head", "seq")),
        P("round", "seq"),
    )
    out_specs = P(("round", "head", "seq"), None)
    return jax.shard_map(shards, mesh=mesh, in_specs=in_specs, out_specs=out_specs, check_vma=False)
```

```python
import functools

import jax
import jax.numpy as jnp
from jax import lax
from jax.experimental import pallas as pl
from jax.experimental.pallas import tpu as pltpu
from jax.sharding import PartitionSpec as P

DH = 128
BLOCK = 1024
TILE = 128
SLOTS = 16
META = 14
SHIFT = 1024

SELF_PENALTY = -100000.0
BUCKET_PENALTY = -1000000000.0
EPSILON = 1e-06
LOWEST = -3.0e38

BF = jnp.bfloat16
F32 = jnp.float32
I32 = jnp.int32
NT = (((1,), (1,)), ((), ()))


def iota(shape, dim):
    return lax.broadcasted_iota(I32, shape, dim)


def mask(cond):
    return jnp.where(cond, 1.0, 0.0).astype(BF)


def mm(a, b):
    return jnp.dot(a, b, preferred_element_type=F32)


def mm_nt(a, b):
    return lax.dot_general(a, b, NT, preferred_element_type=F32)


def full(shape):
    return pl.BlockSpec(shape, lambda *_: (0,) * len(shape))


def slots_of(pos, owners):
    count = pos.shape[1]
    dest = pos >> 10
    hot = iota((owners, count), 0) == dest
    earlier = mask(iota((count, count), 0) < iota((count, count), 1))
    before = mm(mask(hot), earlier)
    rank = jnp.sum(jnp.where(hot, before, 0.0), axis=0, keepdims=True).astype(I32)
    return dest, hot, rank


def pack_kernel(tok_ref, pos_ref, label_ref, out_ref, *, owners):
    count = tok_ref.shape[0]
    width = out_ref.shape[1]
    rows = owners * SLOTS
    tokens = tok_ref[...]
    half = BLOCK // 2
    first, last = label_ref[0:1, 0:1], label_ref[0:1, BLOCK - 1 : BLOCK]
    middle = label_ref[0:1, half - 1 : half]
    marked = jnp.where(last == 0, jnp.minimum(first, middle), jnp.abs(middle - last))
    wide = jnp.where(jnp.broadcast_to(marked, (owners, 128)) == 0, 1.0, 0.0)
    for r in range(2):
        pos = pos_ref[r : r + 1, :]
        dest, hot, rank = slots_of(pos, owners)
        within = pos & (BLOCK - 1)
        slot = dest * SLOTS + rank
        body = mm(mask(iota((rows, count), 0) == slot), tokens)
        value = iota((128, count), 0)
        code = jnp.where((value & 1) == 0, (within >> 5) + 1, within & 31)
        code = jnp.where((value >> 1) == rank, code, 0).astype(F32).astype(BF)
        places = mm_nt(mask(hot), code)
        places = jnp.where(iota((owners, 128), 1) == 2 * SLOTS, wide, places).astype(BF)
        at_meta = mask(iota((rows, owners), 0) == iota((rows, owners), 1) * SLOTS + META)
        extra = mm(at_meta, places)
        for a in range(2):
            at = (a * 2 + r) * rows
            out_ref[at : at + rows, 0:128] = (
                body[:, a * width : a * width + 128] + extra
            ).astype(BF)
            out_ref[at : at + rows, 128:width] = body[
                :, a * width + 128 : (a + 1) * width
            ].astype(BF)


def meta_of(x_ref):
    rows = x_ref.shape[0]
    count = rows // SLOTS
    pick = mask(iota((count, rows), 1) == iota((count, rows), 0) * SLOTS + META)
    return mm(pick, x_ref[:, 0:128]).astype(BF)


def place_rows(meta):
    count = meta.shape[0]
    v, lane = iota((128, 128), 0), iota((128, 128), 1)
    j = lane & (SLOTS - 1)
    weight = jnp.where(v == 2 * j, 32.0, jnp.where(v == 2 * j + 1, 1.0, 0.0)).astype(BF)
    codes = mm(meta, weight)
    own = (iota((count, 128), 0) & 7) == (iota((count, 128), 1) >> 4)
    codes = jnp.where(own, codes, 0.0)
    return jnp.sum(codes.reshape(count // 8, 8, 128), axis=1)


def place_columns(meta, first, rows):
    count = meta.shape[0]
    slot = iota((rows, count), 0) + first
    source = mask((slot >> 4) == iota((rows, count), 1))
    values = mm(source, meta)
    lane = iota((rows, 128), 1)
    keep = (lane >> 1) == (iota((rows, 128), 0) & (SLOTS - 1))
    values = jnp.where(keep, values, 0.0).astype(BF)
    weight = jnp.where((iota((128, 128), 0) & 1) == 0, 32.0, 1.0).astype(BF)
    return mm(values, weight)


def sorted_rows(x_ref, code_ref, out_ref, first):
    step = 256
    chunks = code_ref.shape[0]
    for start in range(0, out_ref.shape[0], step):
        position = (iota((step, 128), 0) + (first + start + 32)).astype(F32)
        picks = [
            mask(position == jnp.broadcast_to(code_ref[q : q + 1, :], (step, 128)))
            for q in range(chunks)
        ]
        picks = jnp.concatenate(picks, axis=1)
        out_ref[start : start + step, :] = mm(picks, x_ref[...]).astype(BF)


def sort_high_kernel(x_ref, high_ref, meta_ref, code_ref, wide_ref):
    meta = meta_of(x_ref)
    meta_ref[...] = meta
    flags = jnp.where(iota(meta.shape, 1) == 2 * SLOTS, meta.astype(F32), 0.0)
    wide_ref[...] = jnp.max(jnp.max(flags, axis=1, keepdims=True), axis=0, keepdims=True)
    code_ref[...] = place_rows(meta)
    sorted_rows(x_ref, code_ref, high_ref, high_ref.shape[0])


def sort_low_kernel(x_ref, code_ref, low_ref):
    sorted_rows(x_ref, code_ref, low_ref, 0)


def project(mine, other, wm, wo):
    return (mm(mine, wm) + mm(other, wo)).astype(BF)


def project_t(mine, other, wm_t, wo_t):
    return (mm_nt(wm_t, mine) + mm_nt(wo_t, other)).astype(BF)


def key_scales(keys):
    sq = jnp.square(keys.astype(F32))
    top = sq.astype(BF)
    rest = (sq - top.astype(F32)).astype(BF)
    total = mm(jnp.concatenate([top, rest], axis=1), jnp.ones((2 * DH, 128), BF))
    return lax.rsqrt(total * (1.0 / DH) + EPSILON) * DH ** (-0.5)


def score_tile(keys, queries, scale, key_label, query_label, diagonal):
    scores = jnp.where(key_label == query_label, mm_nt(keys, queries) * scale, BUCKET_PENALTY)
    if diagonal is None:
        return scores
    cut = scores[diagonal : diagonal + TILE]
    cut = jnp.where(iota((TILE, TILE), 0) == iota((TILE, TILE), 1), SELF_PENALTY, cut)
    parts = [scores[:diagonal]] * (diagonal > 0) + [cut]
    parts += [scores[diagonal + TILE :]] * (diagonal + TILE < scores.shape[0])
    return jnp.concatenate(parts, axis=0) if len(parts) > 1 else cut


def soft(scores, values_t):
    top = jnp.max(scores, axis=0, keepdims=True)
    powers = jnp.exp(scores - top)
    total = jnp.sum(powers, axis=0, keepdims=True)
    return mm(values_t, powers.astype(BF)), top, total


def own_kernel(
    info_ref, lm_ref, hm_ref, lo_ref, ho_ref, wqm_ref, wqo_ref, wvm_ref, wvo_ref,
    row_ref, col_ref, q_ref, out_ref, lse_ref, vt_ref, scale_ref, m_ref, l_ref, acc_ref,
):
    half = lm_ref.shape[0]
    heads = q_ref.shape[1] // DH
    wvm, wvo = jnp.transpose(wvm_ref[...]), jnp.transpose(wvo_ref[...])
    for m_part, o_part, at in ((hm_ref, ho_ref, half), (lm_ref, lo_ref, 0)):
        mine, other = m_part[...], o_part[...]
        keys = project(mine, other, wqm_ref[...], wqo_ref[...])
        q_ref[at : at + half, :] = keys
        for h in range(heads):
            cols = slice(h * DH, (h + 1) * DH)
            scale_ref[at : at + half, cols] = key_scales(keys[:, cols])
        vt_ref[:, at : at + half] = project_t(mine, other, wvm, wvo)
    tiles = BLOCK // TILE
    lse_row = iota((8, TILE), 0)

    def put(at, h, result, total, lse_tile, top):
        out_ref[h * DH : (h + 1) * DH, pl.ds(at, TILE)] = (result * (1.0 / total)).astype(BF)
        return jnp.where(lse_row == h, top + jnp.log(total), lse_tile)

    def band(at, start, size, diagonal):
        query_label = row_ref[0:1, pl.ds(at, TILE)]
        key_label = col_ref[pl.ds(start, size), :]
        lse_tile = jnp.zeros((8, TILE), F32)
        for h in range(heads):
            cols = slice(h * DH, (h + 1) * DH)
            scores = score_tile(
                q_ref[pl.ds(start, size), cols], q_ref[pl.ds(at, TILE), cols],
                scale_ref[pl.ds(start, size), cols], key_label, query_label, diagonal,
            )
            result, top, total = soft(scores, vt_ref[cols, pl.ds(start, size)])
            lse_tile = put(at, h, result, total, lse_tile, top)
        lse_ref[:, pl.ds(at, TILE)] = lse_tile

    @pl.when(info_ref[2] == 0)
    def _():
        band(0, 0, 2 * TILE, 0)

    @pl.loop(1, tiles - 1)
    def _(i):
        @pl.when(info_ref[2 + i] == 0)
        def _():
            at = pl.multiple_of(i * TILE, TILE)
            band(at, pl.multiple_of(at - TILE, TILE), 3 * TILE, TILE)

    @pl.when(info_ref[1 + tiles] == 0)
    def _():
        band(BLOCK - TILE, BLOCK - 2 * TILE, 2 * TILE, TILE)

    @pl.loop(0, tiles)
    def _(i):
        @pl.when(info_ref[2 + i] != 0)
        def _():
            at = pl.multiple_of(i * TILE, TILE)
            query_label = row_ref[0:1, pl.ds(at, TILE)]
            m_ref[...] = jnp.full(m_ref.shape, LOWEST, F32)
            l_ref[...] = jnp.zeros(l_ref.shape, F32)
            acc_ref[...] = jnp.zeros(acc_ref.shape, F32)

            @pl.loop(0, tiles)
            def _(t):
                @pl.when(info_ref[2 + tiles + i * tiles + t] != 0)
                def _():
                    start = pl.multiple_of(t * TILE, TILE)
                    key_label = col_ref[pl.ds(start, TILE), :]
                    apart = iota((TILE, TILE), 0) - iota((TILE, TILE), 1)
                    for h in range(heads):
                        cols = slice(h * DH, (h + 1) * DH)
                        scores = score_tile(
                            q_ref[pl.ds(start, TILE), cols], q_ref[pl.ds(at, TILE), cols],
                            scale_ref[pl.ds(start, TILE), cols], key_label, query_label, None,
                        )
                        scores = jnp.where(apart == at - start, SELF_PENALTY, scores)
                        old = m_ref[h : h + 1, :]
                        top = jnp.maximum(old, jnp.max(scores, axis=0, keepdims=True))
                        powers = jnp.exp(scores - top)
                        shrink = jnp.exp(old - top)
                        m_ref[h : h + 1, :] = top
                        l_ref[h : h + 1, :] = l_ref[h : h + 1, :] * shrink + jnp.sum(
                            powers, axis=0, keepdims=True
                        )
                        acc_ref[cols, :] = acc_ref[cols, :] * shrink + mm(
                            vt_ref[cols, pl.ds(start, TILE)], powers.astype(BF)
                        )

            lse_tile = jnp.zeros((8, TILE), F32)
            for h in range(heads):
                lse_tile = put(
                    at, h, acc_ref[h * DH : (h + 1) * DH, :], l_ref[h : h + 1, :], lse_tile,
                    m_ref[h : h + 1, :],
                )
            lse_ref[:, pl.ds(at, TILE)] = lse_tile


def rest_kernel(
    info_ref, xm_ref, xo_ref, wqm_ref, wqo_ref, wvm_ref, wvo_ref, row_ref, col_ref,
    q_ref, own_ref, own_lse_ref, meta_ref, send_ref,
    out_ref, lse_ref, sums_ref, wvm_t_ref, wvo_t_ref, pk_ref, pv_ref, ps_ref,
):
    halo = xm_ref.shape[0]
    heads = q_ref.shape[1] // DH
    tiles = BLOCK // TILE
    skipped = (BLOCK - halo) // TILE
    meets = 2 + tiles + tiles * tiles
    used = meets + tiles
    out_ref[...] = own_ref[...]
    lse_ref[...] = own_lse_ref[...]
    wvm_t_ref[...] = jnp.transpose(wvm_ref[...])
    wvo_t_ref[...] = jnp.transpose(wvo_ref[...])

    @pl.loop(0, halo // TILE)
    def _(t):
        at = pl.multiple_of(t * TILE, TILE)

        @pl.when(info_ref[used + skipped + t] != 0)
        def _():
            mine, other = xm_ref[pl.ds(at, TILE), :], xo_ref[pl.ds(at, TILE), :]
            keys = project(mine, other, wqm_ref[...], wqo_ref[...])
            pk_ref[pl.ds(at, TILE), :] = keys
            pv_ref[:, pl.ds(at, TILE)] = project_t(mine, other, wvm_t_ref[...], wvo_t_ref[...])
            for h in range(heads):
                cols = slice(h * DH, (h + 1) * DH)
                ps_ref[pl.ds(at, TILE), cols] = key_scales(keys[:, cols])

        @pl.when(info_ref[used + skipped + t] == 0)
        def _():
            pk_ref[pl.ds(at, TILE), :] = jnp.zeros((TILE, heads * DH), BF)
            pv_ref[:, pl.ds(at, TILE)] = jnp.zeros((heads * DH, TILE), BF)
            ps_ref[pl.ds(at, TILE), :] = jnp.zeros((TILE, heads * DH), F32)

    lse_row = iota((8, TILE), 0)

    @pl.loop(0, tiles)
    def _(i):
        @pl.when(info_ref[meets + i] != 0)
        def _():
            at = pl.multiple_of(i * TILE, TILE)
            query_label = row_ref[0:1, pl.ds(at, TILE)]
            lse_tile = lse_ref[:, pl.ds(at, TILE)]
            for h in range(heads):
                cols = slice(h * DH, (h + 1) * DH)
                scores = score_tile(
                    pk_ref[:, cols], q_ref[pl.ds(at, TILE), cols], ps_ref[:, cols],
                    col_ref[BLOCK - halo :, :], query_label, None,
                )
                result, top, total = soft(scores, pv_ref[cols, :])
                there = top + jnp.log(total)
                here = lse_tile[h : h + 1, :]
                largest = jnp.maximum(here, there)
                kept, added = jnp.exp(here - largest), jnp.exp(there - largest)
                merged = kept * out_ref[cols, pl.ds(at, TILE)].astype(F32) + result * (
                    added / total
                )
                out_ref[cols, pl.ds(at, TILE)] = (merged * (1.0 / (kept + added))).astype(BF)
                lse_tile = jnp.where(lse_row == h, largest + jnp.log(kept + added), lse_tile)
            lse_ref[:, pl.ds(at, TILE)] = lse_tile

    row8 = iota((8, BLOCK), 0)
    sums = jnp.zeros((8, BLOCK), F32)
    for h in range(heads):
        lse = lse_ref[h : h + 1, :]
        top = lse.astype(BF).astype(F32)
        sums = jnp.where(row8 == 2 * h, top, jnp.where(row8 == 2 * h + 1, lse - top, sums))
    sums_ref[...] = jnp.concatenate([sums] * SLOTS, axis=0).astype(BF)

    step = 256

    @pl.loop(0, send_ref.shape[0] // step)
    def _(t):
        at = pl.multiple_of(t * step, step)
        codes = place_columns(meta_ref[...], at, step)
        lane = (iota((step, 128), 1) + 32).astype(F32)
        pick = jnp.concatenate(
            [mask(codes == lane + float(c)) for c in range(0, BLOCK, 128)], axis=1
        )
        body = mm_nt(pick, out_ref[...])
        sums = mm_nt(pick, sums_ref[...])
        row = iota((step, 128), 0) & (SLOTS - 1)
        sums = jnp.where(row == (iota((step, 128), 1) >> 3), sums, 0.0)
        sums = jnp.sum(sums.reshape(step // SLOTS, SLOTS, 128), axis=1, keepdims=True)
        sums = jnp.broadcast_to(sums, (step // SLOTS, SLOTS, 128)).reshape(step, 128)
        extra = jnp.where(row == META, sums, 0.0)
        send_ref[pl.ds(at, step), 0:128] = (body[:, 0:128] + extra).astype(BF)
        send_ref[pl.ds(at, step), 128:] = body[:, 128:].astype(BF)


def final_kernel(x_ref, pos_ref, w_ref, out_ref, *, owners):
    count = out_ref.shape[0]
    width = x_ref.shape[1]
    rows = owners * SLOTS
    heads = width // DH
    lane = iota((count, 128), 1)
    picks, meta_picks, ranks = [], [], []
    for r in range(2):
        dest, _, rank = slots_of(pos_ref[r : r + 1, :], owners)
        slot = (dest * SLOTS + rank).astype(F32)
        slot = jnp.transpose(jnp.broadcast_to(slot, (128, count))).astype(I32)
        place = slot & (SLOTS - 1)
        at_meta = slot - place + META
        picks.append(
            jnp.concatenate([mask(slot == lane + c) for c in range(0, rows, 128)], axis=1)
        )
        meta_picks.append(
            jnp.concatenate([mask(at_meta == lane + c) for c in range(0, rows, 128)], axis=1)
        )
        ranks.append(place)
    v = iota((128, width), 0) & 7
    select = mask((v >> 1) == (iota((128, width), 1) >> 7))
    total = None
    for a in range(2):
        values, sums = [], []
        for r in range(2):
            at = (a * 2 + r) * rows
            values.append(mm(picks[r], x_ref[at : at + rows, :]))
            own = mm(meta_picks[r], x_ref[at : at + rows, 0:128])
            own = jnp.where((lane >> 3) == ranks[r], own, 0.0).astype(BF)
            sums.append(mm(own, select))
        largest = jnp.maximum(sums[0], sums[1])
        first, second = jnp.exp(sums[0] - largest), jnp.exp(sums[1] - largest)
        combined = ((first * values[0] + second * values[1]) / (first + second)).astype(BF)
        part = mm(combined, w_ref[a * width : (a + 1) * width, :])
        total = part if total is None else total + part
    out_ref[...] = total.astype(BF)


def window_plan(own, prior):
    first = prior[0]
    own = jnp.where(own < first, own + SHIFT, own).reshape(-1, TILE)
    prior = jnp.where(prior < first, prior + SHIFT, prior).reshape(-1, TILE)
    low, high = jnp.min(own, axis=1), jnp.max(own, axis=1)
    prior_low, prior_high = jnp.min(prior, axis=1), jnp.max(prior, axis=1)

    def meets(key_low, key_high):
        return (key_low[None, :] <= high[:, None]) & (key_high[None, :] >= low[:, None])

    own_meets, prior_meets = meets(low, high), meets(prior_low, prior_high)
    tile = jnp.arange(own.shape[0], dtype=I32)
    beyond = jnp.any(own_meets & (jnp.abs(tile[:, None] - tile[None, :]) > 1), axis=1)
    flags = [beyond, own_meets.reshape(-1), jnp.any(prior_meets, 1), jnp.any(prior_meets, 0)]
    return jnp.concatenate(flags).astype(I32)


def shards(tokens, w_qk, w_v, w_out, positions, buckets):
    tok_dev, model_width = tokens.shape
    owners = lax.axis_size("seq")
    everyone = ("round", "head", "seq")
    total = 2 * 2 * owners
    width = model_width // 2
    heads = width // DH
    rows = total * SLOTS
    half = BLOCK // 2
    core = lax.axis_index("round").astype(I32)
    params = pltpu.CompilerParams(vmem_limit_bytes=48 * 1024 * 1024)

    def shape(*dims, dtype=BF):
        return jax.ShapeDtypeStruct(dims, dtype)

    def cost(flops, moved):
        return pl.CostEstimate(flops=flops, bytes_accessed=moved, transcendentals=0)

    def swap(x):
        return lax.ppermute(x, "round", [(0, 1), (1, 0)])

    def onward(x):
        return lax.ppermute(x, "seq", [(i, (i + 1) % owners) for i in range(owners)])

    def to_round(x, ahead):
        route = []
        for r in range(2):
            for g in range(2):
                for i in range(owners):
                    at = (i + ahead) % owners
                    route.append(((r * 2 + g) * owners + i, (g * 2 + r) * owners + at))
        return lax.ppermute(x, everyone, route)

    def exchange(x):
        x = x.reshape(total, SLOTS, width)
        x = lax.all_to_all(x, everyone, split_axis=0, concat_axis=0, tiled=True)
        return x.reshape(rows, width)

    packed = pl.pallas_call(
        functools.partial(pack_kernel, owners=owners),
        out_shape=shape(rows, width),
        compiler_params=params,
        name="pack",
    )(tokens, positions, buckets)
    arrived = exchange(packed)
    own_label, prior_label = to_round(buckets[0], 0), to_round(buckets[0], 1)

    high, meta, codes, wide = pl.pallas_call(
        sort_high_kernel,
        out_shape=[
            shape(half, width),
            shape(total, 128),
            shape(total // 8, 128, dtype=F32),
            shape(1, 1, dtype=F32),
        ],
        compiler_params=params,
        name="sort_high",
    )(arrived)
    halo_high = onward(high)
    high_other = swap(high)
    low = pl.pallas_call(
        sort_low_kernel,
        out_shape=shape(half, width),
        compiler_params=params,
        cost_estimate=cost(2 * half * rows * width, 4 * 2**20),
        name="sort_low",
    )(arrived, codes)
    low_other = swap(low)

    plan = window_plan(own_label, prior_label)
    info = jnp.concatenate([jnp.stack([core, 1 - core]), plan])
    label_row = own_label[None, :]
    label_col = jnp.broadcast_to(own_label[:, None], (BLOCK, TILE))
    prior_col = jnp.broadcast_to(prior_label[:, None], (BLOCK, TILE))

    def weight(flip):
        return pl.BlockSpec((width, width), lambda i, s: (s[flip], s[0]))

    weights = [weight(0), weight(1), weight(0), weight(1)]
    weight_args = (w_qk, w_qk, w_v, w_v)
    halves = full((half, width))
    queries, own_out, own_lse = pl.pallas_call(
        own_kernel,
        out_shape=[shape(BLOCK, width), shape(width, BLOCK), shape(8, BLOCK, dtype=F32)],
        grid_spec=pltpu.PrefetchScalarGridSpec(
            num_scalar_prefetch=1,
            grid=(1,),
            in_specs=[halves] * 4 + weights + [full((1, BLOCK)), full((BLOCK, TILE))],
            out_specs=[full((BLOCK, width)), full((width, BLOCK)), full((8, BLOCK))],
            scratch_shapes=[
                pltpu.VMEM((width, BLOCK), BF),
                pltpu.VMEM((BLOCK, width), F32),
                pltpu.VMEM((8, TILE), F32),
                pltpu.VMEM((8, TILE), F32),
                pltpu.VMEM((width, TILE), F32),
            ],
        ),
        compiler_params=params,
        cost_estimate=cost(8 * BLOCK * width * width, 8 * 2**20),
        name="own_block",
    )(info, low, high, low_other, high_other, *weight_args, label_row, label_col)
    halo_high, own_lse = lax.optimization_barrier((halo_high, own_lse))

    def finish(halo_mine, halo_other):
        halo = halo_mine.shape[0]
        return pl.pallas_call(
            rest_kernel,
            out_shape=shape(rows, width),
            grid_spec=pltpu.PrefetchScalarGridSpec(
                num_scalar_prefetch=1,
                grid=(1,),
                in_specs=[full((halo, width))] * 2
                + weights
                + [
                    full((1, BLOCK)),
                    full((BLOCK, TILE)),
                    full((BLOCK, width)),
                    full((width, BLOCK)),
                    full((8, BLOCK)),
                    full((total, 128)),
                ],
                out_specs=full((rows, width)),
                scratch_shapes=[
                    pltpu.VMEM((width, BLOCK), BF),
                    pltpu.VMEM((8, BLOCK), F32),
                    pltpu.VMEM((128, BLOCK), BF),
                    pltpu.VMEM((width, width), BF),
                    pltpu.VMEM((width, width), BF),
                    pltpu.VMEM((halo, width), BF),
                    pltpu.VMEM((width, halo), BF),
                    pltpu.VMEM((halo, width), F32),
                ],
            ),
            compiler_params=params,
            name="prior_block",
        )(
            info, halo_mine, halo_other, *weight_args, label_row, prior_col,
            queries, own_out, own_lse, meta,
        )

    halo_high_other = swap(halo_high)

    def whole_window():
        halo_low = onward(low)
        return finish(
            jnp.concatenate([halo_low, halo_high], axis=0),
            jnp.concatenate([swap(halo_low), halo_high_other], axis=0),
        )

    back = lax.cond(
        wide[0, 0] > 0.0, whole_window, lambda: finish(halo_high, halo_high_other)
    )
    returned = exchange(back)
    return pl.pallas_call(
        functools.partial(final_kernel, owners=owners),
        out_shape=shape(tok_dev, model_width),
        compiler_params=params,
        name="combine",
    )(returned, positions, w_out)


def solution(mesh):
    in_specs = (
        P(("round", "head", "seq"), None),
        P(),
        P(),
        P(),
        P(None, ("round", "head", "seq")),
        P("round", "seq"),
    )
    out_specs = P(("round", "head", "seq"), None)
    return jax.shard_map(shards, mesh=mesh, in_specs=in_specs, out_specs=out_specs, check_vma=False)
```

```python
import functools

import jax
import jax.numpy as jnp
from jax import lax
from jax.experimental import pallas as pl
from jax.experimental.pallas import tpu as pltpu
from jax.sharding import PartitionSpec as P

DH = 128
BLOCK = 1024
TILE = 128
SPAN = 256
SPANS = BLOCK // SPAN
SLOTS = 16
META = 14
LABELS = 15
SHIFT = 65536.0
STEP = 256

LOG2E = 1.4426950408889634
SELF_PENALTY = -100000.0 * LOG2E
BUCKET_PENALTY = -1000000000.0
EPSILON = 1e-06

BF = jnp.bfloat16
F32 = jnp.float32
I32 = jnp.int32
NT = (((1,), (1,)), ((), ()))


def iota(shape, dim):
    return lax.broadcasted_iota(I32, shape, dim)


def mask(cond):
    return jnp.where(cond, 1.0, 0.0).astype(BF)


def mm(a, b):
    return jnp.dot(a, b, preferred_element_type=F32)


def mm_nt(a, b):
    return lax.dot_general(a, b, NT, preferred_element_type=F32)


def head_cols(h, wide=1):
    return slice(h * DH * wide, (h + 1) * DH * wide)


def slots_of(pos, owners):
    count = pos.shape[1]
    dest = pos >> 10
    hot = iota((owners, count), 0) == dest
    earlier = mask(iota((count, count), 0) < iota((count, count), 1))
    before = mm(mask(hot), earlier)
    rank = jnp.sum(jnp.where(hot, before, 0.0), axis=0, keepdims=True).astype(I32)
    return hot, dest * SLOTS + rank


def pack_kernel(info_ref, tok_ref, pos_ref, label_ref, out_ref, buf_ref, sem_ref, *, owners):
    count = tok_ref.shape[0]
    width = out_ref.shape[1]
    rows = owners * SLOTS
    tokens = tok_ref[...]
    half = BLOCK // 2
    first, last = label_ref[0:1, 0:1], label_ref[0:1, BLOCK - 1 : BLOCK]
    middle = label_ref[0:1, half - 1 : half]
    marked = jnp.where(last == 0, jnp.minimum(first, middle), jnp.abs(middle - last))
    wide = jnp.where(jnp.broadcast_to(marked, (owners, 128)) == 0, 1.0, 0.0)
    label = label_ref[...]
    label = ((128 + (label & 127)) << (label >> 7)).astype(F32)
    label = jnp.where(info_ref[1] == 0, label[:, :half], label[:, half:])
    label = jnp.broadcast_to(label, (SLOTS, half))
    copies = []
    for r in range(2):
        pos = pos_ref[r : r + 1, :]
        hot, slot = slots_of(pos, owners)
        rank = slot & (SLOTS - 1)
        within = pos & (BLOCK - 1)
        pick = mask(iota((rows, count), 0) == slot)
        value = iota((128, count), 0)
        code = jnp.where((value & 1) == 0, (within >> 5) + 1, within & 31)
        code = jnp.where((value >> 1) == rank, code, 0).astype(F32).astype(BF)
        places = mm_nt(mask(hot), code)
        places = jnp.where(iota((owners, 128), 1) == 2 * SLOTS, wide, places).astype(BF)
        at_meta = mask(iota((rows, owners), 0) == iota((rows, owners), 1) * SLOTS + META)
        extra = mm(at_meta, places)
        for a in range(2):
            at = (a * 2 + r) * rows
            body = mm(pick, tokens[:, a * width : (a + 1) * width])
            buf_ref[at : at + rows, 0:128] = (body[:, 0:128] + extra).astype(BF)
            buf_ref[at : at + rows, 128:width] = body[:, 128:].astype(BF)

        @pl.when(info_ref[0] == r)
        def _():
            for a in range(2):
                for ahead in range(2):
                    block = (info_ref[2] + ahead) & (owners - 1)
                    at = pl.multiple_of((a * 2 + r) * rows + block * SLOTS, SLOTS)
                    old = buf_ref[pl.ds(at, SLOTS), :].astype(F32)
                    new = jnp.where(iota((SLOTS, half), 0) == LABELS, label, old)
                    buf_ref[pl.ds(at, SLOTS), :] = new.astype(BF)

        for a in range(2):
            piece = pl.ds((a * 2 + r) * rows, rows)
            copy = pltpu.make_async_copy(
                buf_ref.at[piece], out_ref.at[piece], sem_ref.at[a * 2 + r]
            )
            copy.start()
            copies.append(copy)
    for copy in copies:
        copy.wait()


def prepare_kernel(
    info_ref, wqm_ref, wqo_ref, wvm_ref, wvo_ref, wo_ref, pos_ref,
    wq_ref, wvt_ref, wout_ref, slot_ref, *, owners,
):
    width = wqm_ref.shape[0]
    wq_ref[0:width, :] = wqm_ref[...]
    wq_ref[width:, :] = wqo_ref[...]
    wvt_ref[:, 0:width] = jnp.transpose(wvm_ref[...])
    wvt_ref[:, width:] = jnp.transpose(wvo_ref[...])
    wout_ref[...] = wo_ref[...]
    count = pos_ref.shape[1]
    for r in range(2):
        slot = slots_of(pos_ref[r : r + 1, :], owners)[1].astype(F32)
        slot_ref[r * count : (r + 1) * count, :] = jnp.transpose(
            jnp.broadcast_to(slot, (128, count))
        )


def meta_of(x_ref):
    rows = x_ref.shape[0]
    count = rows // SLOTS
    pick = mask(iota((count, rows), 1) == iota((count, rows), 0) * SLOTS + META)
    return mm(pick, x_ref[:, 0:128]).astype(BF)


def place_rows(meta):
    count = meta.shape[0]
    v, lane = iota((128, 128), 0), iota((128, 128), 1)
    j = lane & (SLOTS - 1)
    weight = jnp.where(v == 2 * j, 32.0, jnp.where(v == 2 * j + 1, 1.0, 0.0)).astype(BF)
    codes = mm(meta, weight)
    own = (iota((count, 128), 0) & 7) == (iota((count, 128), 1) >> 4)
    codes = jnp.where(own, codes, 0.0)
    return jnp.sum(codes.reshape(count // 8, 8, 128), axis=1)


def place_columns(meta, first, rows):
    count = meta.shape[0]
    slot = iota((rows, count), 0) + first
    source = mask((slot >> 4) == iota((rows, count), 1))
    values = mm(source, meta)
    lane = iota((rows, 128), 1)
    keep = (lane >> 1) == (iota((rows, 128), 0) & (SLOTS - 1))
    values = jnp.where(keep, values, 0.0).astype(BF)
    weight = jnp.where((iota((128, 128), 0) & 1) == 0, 32.0, 1.0).astype(BF)
    return mm(values, weight)


def sorted_rows(x_ref, code_ref, out_ref, first):
    step = 256
    chunks = code_ref.shape[0]
    for start in range(0, out_ref.shape[0], step):
        position = (iota((step, 128), 0) + (first + start + 32)).astype(F32)
        picks = [
            mask(position == jnp.broadcast_to(code_ref[q : q + 1, :], (step, 128)))
            for q in range(chunks)
        ]
        picks = jnp.concatenate(picks, axis=1)
        out_ref[start : start + step, :] = mm(picks, x_ref[...]).astype(BF)


def sort_high_kernel(x_ref, high_ref, meta_ref, code_ref, wide_ref):
    meta = meta_of(x_ref)
    meta_ref[...] = meta
    flags = jnp.where(iota(meta.shape, 1) == 2 * SLOTS, meta.astype(F32), 0.0)
    wide_ref[...] = jnp.max(jnp.max(flags, axis=1, keepdims=True), axis=0, keepdims=True)
    code_ref[...] = place_rows(meta)
    sorted_rows(x_ref, code_ref, high_ref, high_ref.shape[0])


def sort_low_kernel(
    info_ref, x_ref, code_ref, low_ref, row_ref, col_ref, prior_col_ref, flag_ref, *, owners
):
    def labels(block):
        parts = []
        for half in range(2):
            source = (info_ref[1] * 2 + half) * owners + block
            rows = x_ref[pl.ds(pl.multiple_of(source * SLOTS, SLOTS), SLOTS), :].astype(F32)
            at_labels = iota(rows.shape, 0) == LABELS
            parts.append(jnp.sum(jnp.where(at_labels, rows, 0.0), axis=0, keepdims=True))
        return jnp.concatenate(parts, axis=1)

    own = labels(info_ref[2])
    prior = labels((info_ref[2] + owners - 1) & (owners - 1))
    row_ref[...] = own
    col_ref[...] = jnp.transpose(jnp.broadcast_to(own, (TILE, BLOCK)))
    prior_col_ref[...] = jnp.transpose(jnp.broadcast_to(prior, (TILE, BLOCK)))
    flag_ref[...] = jnp.broadcast_to(plan(own, prior), flag_ref.shape)
    sorted_rows(x_ref, code_ref, low_ref, 0)


def plan(own, prior):
    first = prior[:, 0:1]

    def ends(labels):
        labels = jnp.where(labels < first, labels + SHIFT, labels)
        tiles = jnp.concatenate([labels[:, t : t + TILE] for t in range(0, BLOCK, TILE)], axis=0)
        low = jnp.min(tiles, axis=1, keepdims=True)
        high = jnp.max(tiles, axis=1, keepdims=True)
        return jnp.broadcast_to(low, tiles.shape), jnp.broadcast_to(high, tiles.shape)

    low, high = ends(own)
    prior_low, prior_high = ends(prior)
    tile = iota(low.shape, 0)
    bits = jnp.zeros((1, TILE), F32)

    def add(bits, flag, found):
        found = jnp.max(jnp.where(found, 1.0, 0.0), axis=0, keepdims=True)
        return bits + float(2**flag) * found

    per, tiles = SPAN // TILE, BLOCK // TILE
    for i in range(SPANS):
        at = i * per
        span_low = jnp.min(low[at : at + per], axis=0, keepdims=True)
        span_high = jnp.max(high[at : at + per], axis=0, keepdims=True)
        meets = (low <= span_high) & (high >= span_low)
        bits = add(bits, i, meets & ((tile < at - 1) | (tile > at + per)))
        start = min(max(at - 2, 0), tiles - per - 4)
        bits = add(bits, 4 + i, meets & ((tile < start) | (tile >= start + per + 4)))
    some = jnp.zeros(low.shape, F32)
    for i in range(tiles):
        meets = (prior_low <= high[i : i + 1]) & (prior_high >= low[i : i + 1])
        some = jnp.maximum(some, jnp.where(meets, 1.0, 0.0))
        bits = add(bits, 8 + i, meets)
    bits = add(bits, 16, (some > 0.0) & (tile < tiles - 1))
    return add(bits, 17, (some > 0.0) & (tile < tiles - 3))


def flag_bits(flag_ref):
    return jnp.max(flag_ref[...]).astype(I32)


def project(mine, other, wq_ref, wvt_ref):
    width = mine.shape[1]
    queries = (mm(mine, wq_ref[0:width, :]) + mm(other, wq_ref[width:, :])).astype(BF)
    values = mm_nt(wvt_ref[:, 0:width], mine) + mm_nt(wvt_ref[:, width:], other)
    parts = []
    for h in range(queries.shape[1] // DH):
        rows = queries[:, head_cols(h)].astype(F32)
        sq = jnp.square(rows)
        top = sq.astype(BF)
        rest = (sq - top.astype(F32)).astype(BF)
        total = mm(jnp.concatenate([top, rest], axis=1), jnp.ones((2 * DH, 128), BF))
        keys = rows * (lax.rsqrt(total * (1.0 / DH) + EPSILON) * (LOG2E * DH ** (-0.5)))
        top = keys.astype(BF)
        parts += [top, (keys - top.astype(F32)).astype(BF)]
    return queries, parts, values.astype(BF)


def value_rows(h):
    return slice(h * (DH + 16), (h + 1) * (DH + 16))


def store_keys(at, parts, values, key_ref, vt_ref):
    rows = parts[0].shape[0]
    for h in range(len(parts) // 2):
        key_ref[at : at + rows, h * 2 * DH : h * 2 * DH + DH] = parts[2 * h]
        key_ref[at : at + rows, h * 2 * DH + DH : (h + 1) * 2 * DH] = parts[2 * h + 1]
        first = h * (DH + 16)
        vt_ref[first : first + DH, at : at + rows] = values[head_cols(h), :]
        vt_ref[first + DH : first + DH + 16, at : at + rows] = jnp.ones((16, rows), BF)


def attend(keys, queries, values, key_label, query_label, diagonal):
    count, span = keys.shape[0], queries.shape[0]
    scores = mm_nt(keys, jnp.concatenate([queries, queries], axis=1))
    match = jnp.concatenate([key_label] * (span // TILE), axis=1) == query_label
    scores = jnp.where(match, scores, BUCKET_PENALTY)
    if isinstance(diagonal, int):
        cut = scores[diagonal : diagonal + span]
        cut = jnp.where(iota((span, span), 0) == iota((span, span), 1), SELF_PENALTY, cut)
        parts = [scores[:diagonal]] * (diagonal > 0) + [cut]
        parts += [scores[diagonal + span :]] * (diagonal + span < count)
        scores = jnp.concatenate(parts, axis=0) if len(parts) > 1 else cut
    elif diagonal is not None:
        apart = iota((count, span), 0) - iota((count, span), 1)
        scores = jnp.where(apart == diagonal, SELF_PENALTY, scores)
    top = jnp.max(scores, axis=0, keepdims=True)
    result = mm(values, jnp.exp2(scores - top).astype(BF))
    return result[0:DH], top, result[DH : DH + 1]


def sums_of(lse, heads):
    row = iota(lse.shape, 0)
    sums = jnp.zeros(lse.shape, F32)
    for h in range(heads):
        part = lse[h : h + 1, :]
        top = part.astype(BF).astype(F32)
        sums = jnp.where(row == 2 * h, top, jnp.where(row == 2 * h + 1, part - top, sums))
    return jnp.concatenate([sums] * SLOTS, axis=0).astype(BF)


def packed_rows(pick, out, sums):
    body = mm_nt(pick, out)
    sums = mm_nt(pick, sums)
    row = iota((STEP, 128), 0) & (SLOTS - 1)
    sums = jnp.where(row == (iota((STEP, 128), 1) >> 3), sums, 0.0)
    sums = jnp.sum(sums.reshape(STEP // SLOTS, SLOTS, 128), axis=1, keepdims=True)
    sums = jnp.broadcast_to(sums, (STEP // SLOTS, SLOTS, 128)).reshape(STEP, 128)
    extra = jnp.where(row == META, sums, 0.0)
    return jnp.concatenate([body[:, 0:128] + extra, body[:, 128:]], axis=1)


def own_kernel(
    lm_ref, hm_ref, lo_ref, ho_ref, wq_ref, wvt_ref, row_ref, col_ref, flag_ref, meta_ref,
    q_ref, out_ref, lse_ref, place_ref, key_ref, vt_ref,
):
    half = lm_ref.shape[0]
    heads = q_ref.shape[1] // DH
    bits = flag_bits(flag_ref)
    for m_part, o_part, at in ((hm_ref, ho_ref, half), (lm_ref, lo_ref, 0)):
        queries, parts, values = project(m_part[...], o_part[...], wq_ref, wvt_ref)
        q_ref[at : at + half, :] = queries
        store_keys(at, parts, values, key_ref, vt_ref)
    lse_row = iota((8, SPAN), 0)

    def put(at, h, found, lse_tile):
        result, top, total = found
        out_ref[head_cols(h), pl.ds(at, SPAN)] = (result * (1.0 / total)).astype(BF)
        return jnp.where(lse_row == h, top + jnp.log2(total), lse_tile)

    def span(at, start, size, diagonal):
        query_label = row_ref[0:1, pl.ds(at, SPAN)]
        key_label = col_ref[pl.ds(start, size), :]
        lse_tile = jnp.zeros((8, SPAN), F32)
        for h in range(heads):
            found = attend(
                key_ref[pl.ds(start, size), head_cols(h, 2)],
                q_ref[pl.ds(at, SPAN), head_cols(h)],
                vt_ref[value_rows(h), pl.ds(start, size)],
                key_label, query_label, diagonal,
            )
            lse_tile = put(at, h, found, lse_tile)
        lse_ref[:, pl.ds(at, SPAN)] = lse_tile

    def flag(k):
        return (bits >> k) & 1

    @pl.when(flag(0) == 0)
    def _():
        span(0, 0, SPAN + TILE, 0)

    @pl.loop(1, SPANS - 1)
    def _(i):
        @pl.when(flag(i) == 0)
        def _():
            at = pl.multiple_of(i * SPAN, SPAN)
            span(at, pl.multiple_of(at - TILE, TILE), SPAN + 2 * TILE, TILE)

    @pl.when(flag(SPANS - 1) == 0)
    def _():
        span(BLOCK - SPAN, BLOCK - SPAN - TILE, SPAN + TILE, TILE)

    @pl.loop(0, SPANS)
    def _(i):
        at = pl.multiple_of(i * SPAN, SPAN)

        @pl.when((flag(i) != 0) & (flag(4 + i) == 0))
        def _():
            size = SPAN + 4 * TILE
            start = pl.multiple_of(jnp.clip(at - 2 * TILE, 0, BLOCK - size), TILE)
            span(at, start, size, at - start)

        @pl.when(flag(4 + i) != 0)
        def _():
            span(at, 0, BLOCK, at)

    @pl.loop(0, place_ref.shape[0] // STEP)
    def _(t):
        at = pl.multiple_of(t * STEP, STEP)
        place_ref[pl.ds(at, STEP), :] = place_columns(meta_ref[...], at, STEP)


def rest_kernel(
    xm_ref, xo_ref, wq_ref, wvt_ref, row_ref, col_ref, flag_ref,
    q_ref, own_ref, own_lse_ref, place_ref, send_ref,
    out_ref, lse_ref, sums_ref, key_ref, vt_ref, buf_ref, sem_ref,
):
    halo = xm_ref.shape[0]
    heads = q_ref.shape[1] // DH
    bits = flag_bits(flag_ref)
    lse_row = iota((8, TILE), 0)
    out_ref[...] = own_ref[...]
    lse_ref[...] = own_lse_ref[...]

    def merge(size):
        first = halo - size
        _, parts, values = project(xm_ref[first:, :], xo_ref[first:, :], wq_ref, wvt_ref)
        store_keys(first, parts, values, key_ref, vt_ref)

        @pl.loop(0, BLOCK // TILE)
        def _(i):
            @pl.when(((bits >> (8 + i)) & 1) != 0)
            def _():
                at = pl.multiple_of(i * TILE, TILE)
                lse_tile = lse_ref[:, pl.ds(at, TILE)]
                for h in range(heads):
                    result, top, total = attend(
                        key_ref[first:, head_cols(h, 2)],
                        q_ref[pl.ds(at, TILE), head_cols(h)],
                        vt_ref[value_rows(h), first:],
                        col_ref[BLOCK - size :, :], row_ref[0:1, pl.ds(at, TILE)], None,
                    )
                    here, there = lse_tile[h : h + 1, :], top + jnp.log2(total)
                    largest = jnp.maximum(here, there)
                    kept, added = jnp.exp2(here - largest), jnp.exp2(there - largest)
                    own = out_ref[head_cols(h), pl.ds(at, TILE)].astype(F32)
                    merged = (kept * own + result * (added / total)) * (1.0 / (kept + added))
                    out_ref[head_cols(h), pl.ds(at, TILE)] = merged.astype(BF)
                    new = largest + jnp.log2(kept + added)
                    lse_tile = jnp.where(lse_row == h, new, lse_tile)
                lse_ref[:, pl.ds(at, TILE)] = lse_tile

    size_class = bits >> 16

    @pl.when(size_class == 0)
    def _():
        merge(TILE)

    @pl.when(size_class == 1)
    def _():
        merge(3 * TILE)

    @pl.when(size_class > 1)
    def _():
        merge(halo)

    sums_ref[...] = sums_of(lse_ref[...], heads)
    steps = send_ref.shape[0] // STEP

    def sending(t):
        piece = pl.ds(pl.multiple_of(t * STEP, STEP), STEP)
        return pltpu.make_async_copy(buf_ref.at[piece], send_ref.at[piece], sem_ref.at[t])

    @pl.loop(0, steps)
    def _(t):
        at = pl.multiple_of(t * STEP, STEP)
        codes = place_ref[pl.ds(at, STEP), :]
        lane = (iota((STEP, 128), 1) + 32).astype(F32)
        pick = jnp.concatenate(
            [mask(codes == lane + float(c)) for c in range(0, BLOCK, 128)], axis=1
        )
        buf_ref[pl.ds(at, STEP), :] = packed_rows(pick, out_ref[...], sums_ref[...]).astype(BF)
        sending(t).start()

    @pl.loop(0, steps)
    def _(t):
        sending(t).wait()


def final_kernel(x_ref, slot_ref, w_ref, out_ref, *, owners):
    count = out_ref.shape[0]
    width = x_ref.shape[1]
    rows = owners * SLOTS
    lane = iota((count, 128), 1)
    picks, meta_picks, ranks = [], [], []
    for r in range(2):
        slot = slot_ref[r * count : (r + 1) * count, :].astype(I32)
        place = slot & (SLOTS - 1)
        at_meta = slot - place + META
        picks.append(
            jnp.concatenate([mask(slot == lane + c) for c in range(0, rows, 128)], axis=1)
        )
        meta_picks.append(
            jnp.concatenate([mask(at_meta == lane + c) for c in range(0, rows, 128)], axis=1)
        )
        ranks.append(place)
    v = iota((128, width), 0) & 7
    select = mask((v >> 1) == (iota((128, width), 1) >> 7))
    total = None
    for a in range(2):
        values, sums = [], []
        for r in range(2):
            at = (a * 2 + r) * rows
            values.append(mm(picks[r], x_ref[at : at + rows, :]))
            own = mm(meta_picks[r], x_ref[at : at + rows, 0:128])
            own = jnp.where((lane >> 3) == ranks[r], own, 0.0).astype(BF)
            sums.append(mm(own, select))
        largest = jnp.maximum(sums[0], sums[1])
        first, second = jnp.exp2(sums[0] - largest), jnp.exp2(sums[1] - largest)
        combined = ((first * values[0] + second * values[1]) / (first + second)).astype(BF)
        part = mm(combined, w_ref[a * width : (a + 1) * width, :])
        total = part if total is None else total + part
    out_ref[...] = total.astype(BF)


def shards(tokens, w_qk, w_v, w_out, positions, buckets):
    tok_dev, model_width = tokens.shape
    owners = lax.axis_size("seq")
    everyone = ("round", "head", "seq")
    total = 2 * 2 * owners
    width = model_width // 2
    heads = width // DH
    rows = total * SLOTS
    half = BLOCK // 2
    info = jnp.stack([lax.axis_index(axis) for axis in everyone]).astype(I32)
    params = pltpu.CompilerParams(vmem_limit_bytes=40 * 2**20)
    alone = pltpu.CompilerParams(vmem_limit_bytes=60 * 2**20)
    in_vmem = pl.BlockSpec(memory_space=pltpu.VMEM)
    in_smem = pl.BlockSpec(memory_space=pltpu.SMEM)
    in_hbm = pl.BlockSpec(memory_space=pltpu.HBM)

    def shape(*dims, dtype=BF):
        return jax.ShapeDtypeStruct(dims, dtype)

    def cost(flops, moved):
        return pl.CostEstimate(flops=flops, bytes_accessed=moved, transcendentals=0)

    def swap(x):
        return lax.ppermute(x, "round", [(0, 1), (1, 0)])

    def onward(x):
        return lax.ppermute(x, "seq", [(i, (i + 1) % owners) for i in range(owners)])

    def exchange(x):
        x = x.reshape(total, SLOTS, width)
        x = lax.all_to_all(x, everyone, split_axis=0, concat_axis=0, tiled=True)
        return x.reshape(rows, width)

    packed = pl.pallas_call(
        functools.partial(pack_kernel, owners=owners),
        out_shape=shape(rows, width),
        in_specs=[in_smem] + [in_vmem] * 3,
        out_specs=in_hbm,
        scratch_shapes=[pltpu.VMEM((rows, width), BF), pltpu.SemaphoreType.DMA((4,))],
        compiler_params=alone,
        name="pack",
    )(info, tokens, positions, buckets)
    arrived = exchange(packed)

    def weight(other):
        return pl.BlockSpec(
            (width, width), lambda i, s: (1 - s[0] if other else s[0], s[0])
        )

    weights = [weight(False), weight(True)] * 2
    wq, wvt, wout, slots = pl.pallas_call(
        functools.partial(prepare_kernel, owners=owners),
        out_shape=[
            shape(model_width, width),
            shape(width, model_width),
            shape(model_width, model_width),
            shape(2 * tok_dev, 128, dtype=F32),
        ],
        grid_spec=pltpu.PrefetchScalarGridSpec(
            num_scalar_prefetch=1,
            grid=(1,),
            in_specs=weights + [in_vmem] * 2,
            out_specs=[in_vmem] * 4,
        ),
        compiler_params=params,
        cost_estimate=cost(2**30, 8 * 2**20),
        name="prepare",
    )(info, w_qk, w_qk, w_v, w_v, w_out, positions)
    arrived, wq, wvt, wout, slots = lax.optimization_barrier((arrived, wq, wvt, wout, slots))

    high, meta, codes, wide = pl.pallas_call(
        sort_high_kernel,
        out_shape=[
            shape(half, width),
            shape(total, 128),
            shape(total // 8, 128, dtype=F32),
            shape(1, 1, dtype=F32),
        ],
        compiler_params=params,
        name="sort_high",
    )(arrived)
    halo_high = onward(high)
    high_other = swap(high)
    low, label_row, label_col, prior_col, flags = pl.pallas_call(
        functools.partial(sort_low_kernel, owners=owners),
        out_shape=[
            shape(half, width),
            shape(1, BLOCK, dtype=F32),
            shape(BLOCK, TILE, dtype=F32),
            shape(BLOCK, TILE, dtype=F32),
            shape(8, 128, dtype=F32),
        ],
        in_specs=[in_smem] + [in_vmem] * 2,
        out_specs=[in_vmem] * 5,
        compiler_params=params,
        cost_estimate=cost(2 * half * rows * width, 4 * 2**20),
        name="sort_low",
    )(info, arrived, codes)
    low_other = swap(low)

    queries, own_out, own_lse, places = pl.pallas_call(
        own_kernel,
        out_shape=[
            shape(BLOCK, width),
            shape(width, BLOCK),
            shape(8, BLOCK, dtype=F32),
            shape(rows, 128, dtype=F32),
        ],
        in_specs=[in_vmem] * 10,
        out_specs=[in_vmem] * 4,
        scratch_shapes=[
            pltpu.VMEM((BLOCK, 2 * width), BF),
            pltpu.VMEM((heads * (DH + 16), BLOCK), BF),
        ],
        compiler_params=params,
        cost_estimate=cost(8 * BLOCK * width * width, 8 * 2**20),
        name="own_block",
    )(low, high, low_other, high_other, wq, wvt, label_row, label_col, flags, meta)
    halo_high, own_lse = lax.optimization_barrier((halo_high, own_lse))

    def finish(halo_mine, halo_other):
        halo = halo_mine.shape[0]
        return pl.pallas_call(
            rest_kernel,
            out_shape=shape(rows, width),
            in_specs=[in_vmem] * 11,
            out_specs=in_hbm,
            scratch_shapes=[
                pltpu.VMEM((width, BLOCK), BF),
                pltpu.VMEM((8, BLOCK), F32),
                pltpu.VMEM((128, BLOCK), BF),
                pltpu.VMEM((halo, 2 * width), BF),
                pltpu.VMEM((heads * (DH + 16), halo), BF),
                pltpu.VMEM((rows, width), BF),
                pltpu.SemaphoreType.DMA((rows // STEP,)),
            ],
            compiler_params=params,
            name="prior_block",
        )(
            halo_mine, halo_other, wq, wvt, label_row, prior_col, flags,
            queries, own_out, own_lse, places,
        )

    halo_high_other = swap(halo_high)

    def whole_window():
        halo_low = onward(low)
        return finish(
            jnp.concatenate([halo_low, halo_high], axis=0),
            jnp.concatenate([swap(halo_low), halo_high_other], axis=0),
        )

    back = lax.cond(
        wide[0, 0] > 0.0, whole_window, lambda: finish(halo_high, halo_high_other)
    )
    returned = exchange(back)
    return pl.pallas_call(
        functools.partial(final_kernel, owners=owners),
        out_shape=shape(tok_dev, model_width),
        compiler_params=params,
        name="combine",
    )(returned, slots, wout)


def solution(mesh):
    in_specs = (
        P(("round", "head", "seq"), None),
        P(),
        P(),
        P(),
        P(None, ("round", "head", "seq")),
        P("round", "seq"),
    )
    out_specs = P(("round", "head", "seq"), None)
    return jax.shard_map(shards, mesh=mesh, in_specs=in_specs, out_specs=out_specs, check_vma=False)
```

```python
import functools

import jax
import jax.numpy as jnp
from jax import lax
from jax.experimental import pallas as pl
from jax.experimental.pallas import tpu as pltpu
from jax.sharding import PartitionSpec as P

DH = 128
BLOCK = 1024
TILE = 128
SPAN = 256
SPANS = BLOCK // SPAN
SLOTS = 16
META = 14
LABELS = 15
HALO = 3 * TILE
SHIFT = 65536.0
STEP = 1024

LOG2E = 1.4426950408889634
SELF_PENALTY = -100000.0 * LOG2E
BUCKET_PENALTY = -1000000000.0
EPSILON = 1e-06

BF = jnp.bfloat16
F32 = jnp.float32
I32 = jnp.int32
NT = (((1,), (1,)), ((), ()))
AXES = ("round", "head", "seq")


def iota(shape, dim):
    return lax.broadcasted_iota(I32, shape, dim)


def mask(cond):
    return jnp.where(cond, 1.0, 0.0).astype(BF)


def mm(a, b):
    return jnp.dot(a, b, preferred_element_type=F32)


def mm_nt(a, b):
    return lax.dot_general(a, b, NT, preferred_element_type=F32)


def head_cols(h, wide=1):
    return slice(h * DH * wide, (h + 1) * DH * wide)


def chip_of(block):
    y = block >> 3
    ring = (block & 7) ^ ((y & 1) * 7)
    return (y << 3) | (ring & 4) | ((ring & 3) ^ ((ring >> 2) * 3))


def block_of(chip):
    y = chip >> 3
    x = (chip >> 2) & 1
    ring = (x << 2) | ((chip & 3) ^ (x * 3))
    return (y << 3) | (ring ^ ((y & 1) * 7))


def slots_of(pos, owners):
    count = pos.shape[1]
    dest = chip_of(pos >> 10)
    hot = iota((owners, count), 0) == dest
    earlier = mask(iota((count, count), 0) < iota((count, count), 1))
    before = mm(mask(hot), earlier)
    rank = jnp.sum(jnp.where(hot, before, 0.0), axis=0, keepdims=True).astype(I32)
    return hot, dest * SLOTS + rank


def pack_kernel(tok_ref, pos_ref, label_ref, out_ref, buf_ref, sem_ref, *, owners):
    count = tok_ref.shape[0]
    width = out_ref.shape[1]
    rows = owners * SLOTS
    tokens = tok_ref[...]
    half = BLOCK // 2
    first, last = label_ref[0:1, 0:1], label_ref[0:1, BLOCK - 1 : BLOCK]
    wide = []
    for held in (HALO, half):
        middle = label_ref[0:1, BLOCK - held - 1 : BLOCK - held]
        marked = jnp.where(last == 0, jnp.minimum(first, middle), jnp.abs(middle - last))
        wide.append(jnp.where(jnp.broadcast_to(marked, (owners, 128)) == 0, 1.0, 0.0))
    label = label_ref[...]
    label = ((128 + (label & 127)) << (label >> 7)).astype(F32)
    core, head, seq = (lax.axis_index(axis) for axis in AXES)
    label = jnp.where(head == 0, label[:, :half], label[:, half:])
    label = jnp.broadcast_to(label, (SLOTS, half))
    copies = []
    for r in range(2):
        pos = pos_ref[r : r + 1, :]
        hot, slot = slots_of(pos, owners)
        rank = slot & (SLOTS - 1)
        within = pos & (BLOCK - 1)
        pick = mask(iota((rows, count), 0) == slot)
        value = iota((128, count), 0)
        code = jnp.where((value & 1) == 0, (within >> 5) + 1, within & 31)
        code = jnp.where((value >> 1) == rank, code, 0).astype(F32).astype(BF)
        places = mm_nt(mask(hot), code)
        lane = iota((owners, 128), 1)
        places = jnp.where(lane == 2 * SLOTS, wide[0], places)
        places = jnp.where(lane == 2 * SLOTS + 1, wide[1], places).astype(BF)
        at_meta = mask(iota((rows, owners), 0) == iota((rows, owners), 1) * SLOTS + META)
        extra = mm(at_meta, places)
        for a in range(2):
            at = (a * 2 + r) * rows
            body = mm(pick, tokens[:, a * width : (a + 1) * width])
            buf_ref[at : at + rows, 0:128] = (body[:, 0:128] + extra).astype(BF)
            buf_ref[at : at + rows, 128:width] = body[:, 128:].astype(BF)

        @pl.when(core == r)
        def _():
            for a in range(2):
                for ahead in range(2):
                    chip = chip_of((seq + ahead) & (owners - 1))
                    at = pl.multiple_of((a * 2 + r) * rows + chip * SLOTS, SLOTS)
                    old = buf_ref[pl.ds(at, SLOTS), :].astype(F32)
                    new = jnp.where(iota((SLOTS, half), 0) == LABELS, label, old)
                    buf_ref[pl.ds(at, SLOTS), :] = new.astype(BF)

        for a in range(2):
            piece = pl.ds((a * 2 + r) * rows, rows)
            copy = pltpu.make_async_copy(
                buf_ref.at[piece], out_ref.at[piece], sem_ref.at[a * 2 + r]
            )
            copy.start()
            copies.append(copy)
    for copy in copies:
        copy.wait()


def prepare_kernel(
    wqk_ref, wv_ref, wo_ref, pos_ref, wq_ref, wvt_ref, wout_ref, slot_ref,
    wv_buf_ref, sem_ref, *, owners,
):
    width = wq_ref.shape[1]
    core = lax.axis_index("round")
    cols = pl.ds(pl.multiple_of(core * width, width), width)
    copies = [pltpu.make_async_copy(wo_ref, wout_ref, sem_ref.at[4])]
    for part in range(2):
        source = core + part - 2 * part * core
        rows = pl.ds(pl.multiple_of(source * width, width), width)
        there = pl.ds(part * width, width)
        copies += [
            pltpu.make_async_copy(wqk_ref.at[rows, cols], wq_ref.at[there], sem_ref.at[part]),
            pltpu.make_async_copy(wv_ref.at[rows, cols], wv_buf_ref.at[there], sem_ref.at[2 + part]),
        ]
    for copy in copies:
        copy.start()
    count = pos_ref.shape[1]
    for r in range(2):
        slot = slots_of(pos_ref[r : r + 1, :], owners)[1].astype(F32)
        slot_ref[r * count : (r + 1) * count, :] = jnp.transpose(
            jnp.broadcast_to(slot, (128, count))
        )
    for copy in copies:
        copy.wait()
    wvt_ref[...] = jnp.transpose(wv_buf_ref[...])


def meta_of(x_ref):
    rows = x_ref.shape[0]
    count = rows // SLOTS
    pick = mask(iota((count, rows), 1) == iota((count, rows), 0) * SLOTS + META)
    return mm(pick, x_ref[:, 0:128]).astype(BF)


def place_rows(meta):
    count = meta.shape[0]
    v, lane = iota((128, 128), 0), iota((128, 128), 1)
    j = lane & (SLOTS - 1)
    weight = jnp.where(v == 2 * j, 32.0, jnp.where(v == 2 * j + 1, 1.0, 0.0)).astype(BF)
    codes = mm(meta, weight)
    own = (iota((count, 128), 0) & 7) == (iota((count, 128), 1) >> 4)
    codes = jnp.where(own, codes, 0.0)
    return jnp.sum(codes.reshape(count // 8, 8, 128), axis=1)


def place_columns(meta):
    count = meta.shape[0]
    rows = count * SLOTS
    values = jnp.broadcast_to(meta.astype(F32)[:, None, :], (count, SLOTS, 128))
    keep = (iota((rows, 128), 1) >> 1) == (iota((rows, 128), 0) & (SLOTS - 1))
    values = jnp.where(keep, values.reshape(rows, 128), 0.0).astype(BF)
    weight = jnp.where((iota((128, 128), 0) & 1) == 0, 32.0, 1.0).astype(BF)
    return mm(values, weight)


def sorted_rows(x_ref, code_ref, out_ref, first):
    rows = out_ref.shape[0]
    position = (iota((rows, 128), 0) + (first + 32)).astype(F32)
    picks = [
        mask(position == jnp.broadcast_to(code_ref[q : q + 1, :], (rows, 128)))
        for q in range(code_ref.shape[0])
    ]
    out_ref[...] = mm(jnp.concatenate(picks, axis=1), x_ref[...]).astype(BF)


def sort_high_kernel(x_ref, high_ref, meta_ref, code_ref, wide_ref):
    meta = meta_of(x_ref)
    meta_ref[...] = meta
    lane = iota(meta.shape, 1)
    flags = jnp.where((lane >> 1) == SLOTS, meta.astype(F32), 0.0)
    flags = jnp.max(flags, axis=0, keepdims=True)
    wide_ref[...] = jnp.sum(flags, axis=1, keepdims=True)
    code_ref[...] = place_rows(meta)
    sorted_rows(x_ref, code_ref, high_ref, BLOCK - high_ref.shape[0])


def sort_low_kernel(
    x_ref, code_ref, low_ref, row_ref, col_ref, prior_col_ref, flag_ref, *, owners
):
    my_round, me = lax.axis_index("head"), block_of(lax.axis_index("seq"))

    def labels(block):
        parts = []
        for half in range(2):
            source = (my_round * 2 + half) * owners + block
            rows = x_ref[pl.ds(pl.multiple_of(source * SLOTS, SLOTS), SLOTS), :].astype(F32)
            at_labels = iota(rows.shape, 0) == LABELS
            parts.append(jnp.sum(jnp.where(at_labels, rows, 0.0), axis=0, keepdims=True))
        return jnp.concatenate(parts, axis=1)

    own = labels(me)
    prior = labels((me + owners - 1) & (owners - 1))
    row_ref[...] = own
    col_ref[...] = jnp.transpose(jnp.broadcast_to(own, (TILE, BLOCK)))
    prior_col_ref[...] = jnp.transpose(jnp.broadcast_to(prior, (TILE, BLOCK)))
    flag_ref[...] = jnp.broadcast_to(plan(own, prior), flag_ref.shape)
    sorted_rows(x_ref, code_ref, low_ref, 0)


def plan(own, prior):
    first = prior[:, 0:1]

    def ends(labels):
        labels = jnp.where(labels < first, labels + SHIFT, labels)
        tiles = jnp.concatenate([labels[:, t : t + TILE] for t in range(0, BLOCK, TILE)], axis=0)
        low = jnp.min(tiles, axis=1, keepdims=True)
        high = jnp.max(tiles, axis=1, keepdims=True)
        return jnp.broadcast_to(low, tiles.shape), jnp.broadcast_to(high, tiles.shape)

    low, high = ends(own)
    prior_low, prior_high = ends(prior)
    tile = iota(low.shape, 0)
    bits = jnp.zeros((1, TILE), F32)

    def add(bits, flag, found):
        found = jnp.max(jnp.where(found, 1.0, 0.0), axis=0, keepdims=True)
        return bits + float(2**flag) * found

    per, tiles = SPAN // TILE, BLOCK // TILE
    for i in range(SPANS):
        at = i * per
        span_low = jnp.min(low[at : at + per], axis=0, keepdims=True)
        span_high = jnp.max(high[at : at + per], axis=0, keepdims=True)
        meets = (low <= span_high) & (high >= span_low)
        bits = add(bits, i, meets & ((tile < at - 1) | (tile > at + per)))
        start = min(max(at - 2, 0), tiles - per - 4)
        bits = add(bits, 4 + i, meets & ((tile < start) | (tile >= start + per + 4)))
    some = jnp.zeros(low.shape, F32)
    for i in range(tiles):
        meets = (prior_low <= high[i : i + 1]) & (prior_high >= low[i : i + 1])
        some = jnp.maximum(some, jnp.where(meets, 1.0, 0.0))
        bits = add(bits, 8 + i, meets)
    bits = add(bits, 16, (some > 0.0) & (tile < tiles - 1))
    return add(bits, 17, (some > 0.0) & (tile < tiles - 3))


def flag_bits(flag_ref):
    return jnp.max(flag_ref[...]).astype(I32)


def project(mine, other, wq_ref, wvt_ref):
    width = mine.shape[1]
    queries = (mm(mine, wq_ref[0:width, :]) + mm(other, wq_ref[width:, :])).astype(BF)
    values = mm_nt(wvt_ref[:, 0:width], mine) + mm_nt(wvt_ref[:, width:], other)
    parts = []
    for h in range(queries.shape[1] // DH):
        rows = queries[:, head_cols(h)].astype(F32)
        sq = jnp.square(rows)
        top = sq.astype(BF)
        rest = (sq - top.astype(F32)).astype(BF)
        total = mm(jnp.concatenate([top, rest], axis=1), jnp.ones((2 * DH, 128), BF))
        keys = rows * (lax.rsqrt(total * (1.0 / DH) + EPSILON) * (LOG2E * DH ** (-0.5)))
        top = keys.astype(BF)
        parts += [top, (keys - top.astype(F32)).astype(BF)]
    return queries, parts, values.astype(BF)


def value_rows(h):
    return slice(h * (DH + 16), (h + 1) * (DH + 16))


def store_keys(at, parts, values, key_ref, vt_ref):
    rows = parts[0].shape[0]
    for h in range(len(parts) // 2):
        key_ref[at : at + rows, h * 2 * DH : h * 2 * DH + DH] = parts[2 * h]
        key_ref[at : at + rows, h * 2 * DH + DH : (h + 1) * 2 * DH] = parts[2 * h + 1]
        first = h * (DH + 16)
        vt_ref[first : first + DH, at : at + rows] = values[head_cols(h), :]
        vt_ref[first + DH : first + DH + 16, at : at + rows] = jnp.ones((16, rows), BF)


def score(keys, queries, key_label, query_label, diagonal):
    count, span = keys.shape[0], queries.shape[0]
    scores = mm_nt(keys, jnp.concatenate([queries, queries], axis=1))
    match = jnp.concatenate([key_label] * (span // TILE), axis=1) == query_label
    scores = jnp.where(match, scores, BUCKET_PENALTY)
    if isinstance(diagonal, int):
        cut = scores[diagonal : diagonal + span]
        cut = jnp.where(iota((span, span), 0) == iota((span, span), 1), SELF_PENALTY, cut)
        parts = [scores[:diagonal]] * (diagonal > 0) + [cut]
        parts += [scores[diagonal + span :]] * (diagonal + span < count)
        scores = jnp.concatenate(parts, axis=0) if len(parts) > 1 else cut
    elif diagonal is not None:
        apart = iota((count, span), 0) - iota((count, span), 1)
        scores = jnp.where(apart == diagonal, SELF_PENALTY, scores)
    return scores


def weigh(scores, values):
    top = jnp.max(scores, axis=0, keepdims=True)
    result = mm(values, jnp.exp2(scores - top).astype(BF))
    return result[0:DH], top, result[DH : DH + 1]


def ahead(work, first, second, depth):
    pending = []
    for item in work:
        pending.append((item, first(item)))
        if len(pending) > depth:
            second(*pending.pop(0))
    for entry in pending:
        second(*entry)


def late_span(bits, i):
    return ((bits >> (8 + SPAN // TILE * i)) & (2 ** (SPAN // TILE) - 1)) != 0


def sums_of(lse, heads):
    row = iota(lse.shape, 0)
    sums = jnp.zeros(lse.shape, F32)
    for h in range(heads):
        part = lse[h : h + 1, :]
        top = part.astype(BF).astype(F32)
        sums = jnp.where(row == 2 * h, top, jnp.where(row == 2 * h + 1, part - top, sums))
    return jnp.concatenate([sums] * SLOTS, axis=0).astype(BF)


def packed_rows(pick, out, sums):
    body = mm_nt(pick, out)
    sums = mm_nt(pick, sums)
    row = iota((STEP, 128), 0) & (SLOTS - 1)
    sums = jnp.where(row == (iota((STEP, 128), 1) >> 3), sums, 0.0)
    sums = jnp.sum(sums.reshape(STEP // SLOTS, SLOTS, 128), axis=1, keepdims=True)
    sums = jnp.broadcast_to(sums, (STEP // SLOTS, SLOTS, 128)).reshape(STEP, 128)
    extra = jnp.where(row == META, sums, 0.0)
    return jnp.concatenate([body[:, 0:128] + extra, body[:, 128:]], axis=1)


def own_kernel(
    lm_ref, hm_ref, lo_ref, ho_ref, wq_ref, wvt_ref, row_ref, col_ref, flag_ref, meta_ref,
    q_ref, out_ref, lse_ref, place_ref, early_ref, key_ref, vt_ref,
):
    first_rows = lm_ref.shape[0]
    heads = q_ref.shape[1] // DH
    bits = flag_bits(flag_ref)
    for m_part, o_part, at in ((hm_ref, ho_ref, first_rows), (lm_ref, lo_ref, 0)):
        queries, parts, values = project(m_part[...], o_part[...], wq_ref, wvt_ref)
        q_ref[at : at + queries.shape[0], :] = queries
        store_keys(at, parts, values, key_ref, vt_ref)
    place_ref[...] = place_columns(meta_ref[...])
    lse_row = iota((8, SPAN), 0)

    def spans(work, depth):
        tiles = {}

        def first(item):
            h, at, start, size, diagonal = item
            return score(
                key_ref[pl.ds(start, size), head_cols(h, 2)], q_ref[pl.ds(at, SPAN), head_cols(h)],
                col_ref[pl.ds(start, size), :], row_ref[0:1, pl.ds(at, SPAN)], diagonal,
            )

        def second(item, scores):
            h, at, start, size, _ = item
            result, top, total = weigh(scores, vt_ref[value_rows(h), pl.ds(start, size)])
            out_ref[head_cols(h), pl.ds(at, SPAN)] = (result * (1.0 / total)).astype(BF)
            tile = tiles.pop("lse") if h else jnp.zeros((8, SPAN), F32)
            tiles["lse"] = jnp.where(lse_row == h, top + jnp.log2(total), tile)
            if h == heads - 1:
                lse_ref[:, pl.ds(at, SPAN)] = tiles.pop("lse")

        ahead(work, first, second, depth)

    work = []
    for at in range(BLOCK - SPAN, -1, -SPAN):
        start, stop = max(at - TILE, 0), min(at + SPAN + TILE, BLOCK)
        work += [(h, at, start, stop - start, at - start) for h in range(heads)]
    spans(work, 3)

    def flag(k):
        return (bits >> k) & 1

    @pl.loop(0, SPANS)
    def _(i):
        at = pl.multiple_of(i * SPAN, SPAN)

        @pl.when((flag(i) != 0) & (flag(4 + i) == 0))
        def _():
            size = SPAN + 4 * TILE
            start = pl.multiple_of(jnp.clip(at - 2 * TILE, 0, BLOCK - size), TILE)
            spans([(h, at, start, size, at - start) for h in range(heads)], 2)

        @pl.when(flag(4 + i) != 0)
        def _():
            spans([(h, at, 0, BLOCK, at) for h in range(heads)], 0)

    late = [jnp.where(late_span(bits, i), 4.0 * BLOCK, 0.0) for i in range(SPANS)]
    sums = sums_of(lse_ref[...], heads)
    for at in range(0, early_ref.shape[0], STEP):
        codes = place_ref[at : at + STEP, :]
        lane = (iota((STEP, 128), 1) + 32).astype(F32)
        pick = jnp.concatenate(
            [mask(codes == lane + (float(c) + late[c // SPAN])) for c in range(0, BLOCK, 128)],
            axis=1,
        )
        early_ref[at : at + STEP, :] = packed_rows(pick, out_ref[...], sums).astype(BF)


def rest_kernel(
    xm_ref, xo_ref, wq_ref, wvt_ref, row_ref, col_ref, flag_ref,
    q_ref, own_ref, own_lse_ref, place_ref, early_ref, send_ref,
    out_ref, lse_ref, key_ref, vt_ref, buf_ref, sem_ref,
):
    halo = xm_ref.shape[0]
    heads = q_ref.shape[1] // DH
    bits = flag_bits(flag_ref)
    lse_row = iota((8, TILE), 0)
    lse_ref[...] = own_lse_ref[...]
    for i in range(SPANS):

        @pl.when(late_span(bits, i))
        def _():
            out_ref[:, i * SPAN : (i + 1) * SPAN] = own_ref[:, i * SPAN : (i + 1) * SPAN]

    def merge(size):
        first = halo - size
        _, parts, values = project(xm_ref[first:, :], xo_ref[first:, :], wq_ref, wvt_ref)
        store_keys(first, parts, values, key_ref, vt_ref)

        @pl.loop(0, BLOCK // TILE)
        def _(i):
            @pl.when(((bits >> (8 + i)) & 1) != 0)
            def _():
                at = pl.multiple_of(i * TILE, TILE)
                tiles = [lse_ref[:, pl.ds(at, TILE)]]

                def first_step(h):
                    return score(
                        key_ref[first:, head_cols(h, 2)], q_ref[pl.ds(at, TILE), head_cols(h)],
                        col_ref[BLOCK - size :, :], row_ref[0:1, pl.ds(at, TILE)], None,
                    )

                def second_step(h, scores):
                    result, top, total = weigh(scores, vt_ref[value_rows(h), first:])
                    here, there = tiles[0][h : h + 1, :], top + jnp.log2(total)
                    largest = jnp.maximum(here, there)
                    kept, added = jnp.exp2(here - largest), jnp.exp2(there - largest)
                    own = out_ref[head_cols(h), pl.ds(at, TILE)].astype(F32)
                    merged = (kept * own + result * (added / total)) * (1.0 / (kept + added))
                    out_ref[head_cols(h), pl.ds(at, TILE)] = merged.astype(BF)
                    new = largest + jnp.log2(kept + added)
                    tiles[0] = jnp.where(lse_row == h, new, tiles[0])

                ahead(range(heads), first_step, second_step, 3)
                lse_ref[:, pl.ds(at, TILE)] = tiles[0]

    if halo > HALO:
        merge(halo)
    else:
        pl.when(bits >> 16 == 0)(lambda: merge(TILE))
        pl.when(bits >> 16 != 0)(lambda: merge(halo))

    copies = []
    for t in range(send_ref.shape[0] // STEP):
        piece = pl.ds(t * STEP, STEP)
        buf_ref[piece, :] = early_ref[piece, :]

        @pl.loop(0, SPANS)
        def _(i):
            @pl.when(late_span(bits, i))
            def _():
                cols = pl.ds(pl.multiple_of(i * SPAN, SPAN), SPAN)
                codes = place_ref[piece, :]
                lane = (iota((STEP, 128), 1) + (32 + i * SPAN)).astype(F32)
                pick = jnp.concatenate(
                    [mask(codes == lane + float(c)) for c in range(0, SPAN, 128)], axis=1
                )
                rows = packed_rows(pick, out_ref[:, cols], sums_of(lse_ref[:, cols], heads))
                buf_ref[piece, :] = (buf_ref[piece, :].astype(F32) + rows).astype(BF)

        copies.append(pltpu.make_async_copy(buf_ref.at[piece], send_ref.at[piece], sem_ref.at[t]))
        copies[-1].start()
    for copy in copies:
        copy.wait()


def final_kernel(x_ref, slot_ref, w_ref, out_ref, *, owners):
    count = out_ref.shape[0]
    width = x_ref.shape[1]
    rows = owners * SLOTS
    lane = iota((count, 128), 1)
    picks, meta_picks, ranks = [], [], []
    for r in range(2):
        slot = slot_ref[r * count : (r + 1) * count, :].astype(I32)
        place = slot & (SLOTS - 1)
        at_meta = slot - place + META
        picks.append(
            jnp.concatenate([mask(slot == lane + c) for c in range(0, rows, 128)], axis=1)
        )
        meta_picks.append(
            jnp.concatenate([mask(at_meta == lane + c) for c in range(0, rows, 128)], axis=1)
        )
        ranks.append(place)
    v = iota((128, width), 0) & 7
    select = mask((v >> 1) == (iota((128, width), 1) >> 7))
    total = None
    for a in range(2):
        values, sums = [], []
        for r in range(2):
            at = (a * 2 + r) * rows
            values.append(mm(picks[r], x_ref[at : at + rows, :]))
            own = mm(meta_picks[r], x_ref[at : at + rows, 0:128])
            own = jnp.where((lane >> 3) == ranks[r], own, 0.0).astype(BF)
            sums.append(mm(own, select))
        largest = jnp.maximum(sums[0], sums[1])
        first, second = jnp.exp2(sums[0] - largest), jnp.exp2(sums[1] - largest)
        combined = ((first * values[0] + second * values[1]) / (first + second)).astype(BF)
        part = mm(combined, w_ref[a * width : (a + 1) * width, :])
        total = part if total is None else total + part
    out_ref[...] = total.astype(BF)


def shards(tokens, w_qk, w_v, w_out, positions, buckets):
    tok_dev, model_width = tokens.shape
    owners = lax.axis_size("seq")
    total = 2 * 2 * owners
    width = model_width // 2
    heads = width // DH
    rows = total * SLOTS
    params = pltpu.CompilerParams(vmem_limit_bytes=40 * 2**20)
    alone = pltpu.CompilerParams(vmem_limit_bytes=60 * 2**20)
    in_vmem = pl.BlockSpec(memory_space=pltpu.VMEM)
    in_hbm = pl.BlockSpec(memory_space=pltpu.HBM)

    def shape(*dims, dtype=BF):
        return jax.ShapeDtypeStruct(dims, dtype)

    def cost(flops, moved):
        return pl.CostEstimate(flops=flops, bytes_accessed=moved, transcendentals=0)

    def swap(x):
        return lax.ppermute(x, "round", [(0, 1), (1, 0)])

    def onward(x):
        route = [(chip_of(i), chip_of((i + 1) % owners)) for i in range(owners)]
        return lax.ppermute(x, "seq", route)

    def exchange(x):
        x = x.reshape(total, SLOTS, width)
        x = lax.all_to_all(x, AXES, split_axis=0, concat_axis=0, tiled=True)
        return x.reshape(rows, width)

    packed = pl.pallas_call(
        functools.partial(pack_kernel, owners=owners),
        out_shape=shape(rows, width),
        out_specs=in_hbm,
        scratch_shapes=[pltpu.VMEM((rows, width), BF), pltpu.SemaphoreType.DMA((4,))],
        compiler_params=alone,
        name="pack",
    )(tokens, positions, buckets)
    arrived = exchange(packed)

    wq, wvt, wout, slots = pl.pallas_call(
        functools.partial(prepare_kernel, owners=owners),
        out_shape=[
            shape(model_width, width),
            shape(width, model_width),
            shape(model_width, model_width),
            shape(2 * tok_dev, 128, dtype=F32),
        ],
        in_specs=[in_hbm] * 3 + [in_vmem],
        out_specs=[in_vmem] * 4,
        scratch_shapes=[pltpu.VMEM((model_width, width), BF), pltpu.SemaphoreType.DMA((5,))],
        compiler_params=params,
        cost_estimate=cost(2**30, 8 * 2**20),
        name="prepare",
    )(w_qk, w_v, w_out, positions)
    arrived, wq, wvt, wout, slots = lax.optimization_barrier((arrived, wq, wvt, wout, slots))

    high, meta, codes, wide = pl.pallas_call(
        sort_high_kernel,
        out_shape=[
            shape(HALO, width),
            shape(total, 128),
            shape(total // 8, 128, dtype=F32),
            shape(1, 1, dtype=F32),
        ],
        compiler_params=params,
        name="sort_high",
    )(arrived)
    halo = onward(high)
    high_other = swap(high)
    low, label_row, label_col, prior_col, flags = pl.pallas_call(
        functools.partial(sort_low_kernel, owners=owners),
        out_shape=[
            shape(BLOCK - HALO, width),
            shape(1, BLOCK, dtype=F32),
            shape(BLOCK, TILE, dtype=F32),
            shape(BLOCK, TILE, dtype=F32),
            shape(8, 128, dtype=F32),
        ],
        compiler_params=params,
        cost_estimate=cost(4 * BLOCK * rows * width, 4 * 2**20),
        name="sort_low",
    )(arrived, codes)
    low_other = swap(low)

    queries, own_out, own_lse, places, early = pl.pallas_call(
        own_kernel,
        out_shape=[
            shape(BLOCK, width),
            shape(width, BLOCK),
            shape(8, BLOCK, dtype=F32),
            shape(rows, 128, dtype=F32),
            shape(rows, width),
        ],
        in_specs=[in_vmem] * 10,
        out_specs=[in_vmem] * 5,
        scratch_shapes=[
            pltpu.VMEM((BLOCK, 2 * width), BF),
            pltpu.VMEM((heads * (DH + 16), BLOCK), BF),
        ],
        compiler_params=params,
        cost_estimate=cost(2**20, 2**20),
        name="own_block",
    )(low, high, low_other, high_other, wq, wvt, label_row, label_col, flags, meta)
    halo, own_lse = lax.optimization_barrier((halo, own_lse))

    def finish(halo_mine, halo_other):
        size = halo_mine.shape[0]
        return pl.pallas_call(
            rest_kernel,
            out_shape=shape(rows, width),
            in_specs=[in_vmem] * 12,
            out_specs=in_hbm,
            scratch_shapes=[
                pltpu.VMEM((width, BLOCK), BF),
                pltpu.VMEM((8, BLOCK), F32),
                pltpu.VMEM((size, 2 * width), BF),
                pltpu.VMEM((heads * (DH + 16), size), BF),
                pltpu.VMEM((rows, width), BF),
                pltpu.SemaphoreType.DMA((rows // STEP,)),
            ],
            compiler_params=params,
            name="prior_block",
        )(
            halo_mine, halo_other, wq, wvt, label_row, prior_col, flags,
            queries, own_out, own_lse, places, early,
        )

    halo_other = swap(halo)

    def more(rows):
        rest = onward(rows)
        return finish(
            jnp.concatenate([rest, halo], axis=0),
            jnp.concatenate([swap(rest), halo_other], axis=0),
        )

    back = lax.cond(wide[0, 0] > 0.0, lambda: more(low), lambda: finish(halo, halo_other))
    returned = exchange(back)
    return pl.pallas_call(
        functools.partial(final_kernel, owners=owners),
        out_shape=shape(tok_dev, model_width),
        compiler_params=params,
        name="combine",
    )(returned, slots, wout)


def solution(mesh):
    in_specs = (
        P(("round", "head", "seq"), None),
        P(),
        P(),
        P(),
        P(None, ("round", "head", "seq")),
        P("round", "seq"),
    )
    out_specs = P(("round", "head", "seq"), None)
    return jax.shard_map(shards, mesh=mesh, in_specs=in_specs, out_specs=out_specs, check_vma=False)
```

```python
import functools

import jax
import jax.numpy as jnp
from jax import lax
from jax.experimental import pallas as pl
from jax.experimental.pallas import tpu as pltpu
from jax.sharding import PartitionSpec as P

DH = 128
BLOCK = 1024
TILE = 128
SPAN = 256
SPANS = BLOCK // SPAN
SLOTS = 16
META = 14
LABELS = 15
HALO = 3 * TILE
SHIFT = 65536.0
STEP = 1024
PIECE = 512

LOG2E = 1.4426950408889634
SELF_PENALTY = -100000.0 * LOG2E
BUCKET_PENALTY = -1000000000.0
EPSILON = 1e-06

BF = jnp.bfloat16
F32 = jnp.float32
I32 = jnp.int32
NT = (((1,), (1,)), ((), ()))
AXES = ("round", "head", "seq")


def iota(shape, dim):
    return lax.broadcasted_iota(I32, shape, dim)


def mask(cond):
    return jnp.where(cond, 1.0, 0.0).astype(BF)


def mm(a, b):
    return jnp.dot(a, b, preferred_element_type=F32)


def mm_nt(a, b):
    return lax.dot_general(a, b, NT, preferred_element_type=F32)


def head_cols(h, wide=1):
    return slice(h * DH * wide, (h + 1) * DH * wide)


def chip_of(block):
    y = block >> 3
    ring = (block & 7) ^ ((y & 1) * 7)
    return (y << 3) | (ring & 4) | ((ring & 3) ^ ((ring >> 2) * 3))


def block_of(chip):
    y = chip >> 3
    x = (chip >> 2) & 1
    ring = (x << 2) | ((chip & 3) ^ (x * 3))
    return (y << 3) | (ring ^ ((y & 1) * 7))


def slots_of(pos, owners):
    count = pos.shape[1]
    dest = chip_of(pos >> 10)
    hot = iota((owners, count), 0) == dest
    earlier = mask(iota((count, count), 0) < iota((count, count), 1))
    before = mm(mask(hot), earlier)
    rank = jnp.sum(jnp.where(hot, before, 0.0), axis=0, keepdims=True).astype(I32)
    return hot, dest * SLOTS + rank


def pack_kernel(
    tok_hbm_ref, pos_ref, label_ref, out_ref, tok_ref, buf_ref, in_sem, sem_ref, *, owners
):
    count = tok_ref.shape[0]
    width = out_ref.shape[1]
    rows = owners * SLOTS
    half = BLOCK // 2
    loads = []
    for a in range(2):
        cols = pl.ds(a * width, width)
        loads.append(
            pltpu.make_async_copy(tok_hbm_ref.at[:, cols], tok_ref.at[:, cols], in_sem.at[a])
        )
        loads[-1].start()
    first, last = label_ref[0:1, 0:1], label_ref[0:1, BLOCK - 1 : BLOCK]
    wide = []
    for held in (HALO, half):
        middle = label_ref[0:1, BLOCK - held - 1 : BLOCK - held]
        marked = jnp.where(last == 0, jnp.minimum(first, middle), jnp.abs(middle - last))
        wide.append(jnp.where(jnp.broadcast_to(marked, (owners, 128)) == 0, 1.0, 0.0))
    label = label_ref[...]
    label = ((128 + (label & 127)) << (label >> 7)).astype(F32)
    core, head, seq = (lax.axis_index(axis) for axis in AXES)
    label = jnp.where(head == 0, label[:, :half], label[:, half:])
    label = jnp.broadcast_to(label, (SLOTS, half))
    picks, extras = [], []
    for r in range(2):
        pos = pos_ref[r : r + 1, :]
        hot, slot = slots_of(pos, owners)
        rank = slot & (SLOTS - 1)
        within = pos & (BLOCK - 1)
        picks.append(mask(iota((rows, count), 0) == slot))
        value = iota((128, count), 0)
        code = jnp.where((value & 1) == 0, (within >> 5) + 1, within & 31)
        code = jnp.where((value >> 1) == rank, code, 0).astype(F32).astype(BF)
        places = mm_nt(mask(hot), code)
        lane = iota((owners, 128), 1)
        places = jnp.where(lane == 2 * SLOTS, wide[0], places)
        places = jnp.where(lane == 2 * SLOTS + 1, wide[1], places).astype(BF)
        at_meta = mask(iota((rows, owners), 0) == iota((rows, owners), 1) * SLOTS + META)
        extras.append(mm(at_meta, places))
    copies = []
    for a in range(2):
        loads[a].wait()
        for r in range(2):
            at = (a * 2 + r) * rows
            body = mm(picks[r], tok_ref[:, a * width : (a + 1) * width])
            buf_ref[at : at + rows, 0:128] = (body[:, 0:128] + extras[r]).astype(BF)
            buf_ref[at : at + rows, 128:width] = body[:, 128:].astype(BF)

            @pl.when(core == r)
            def _():
                for step in range(2):
                    chip = chip_of((seq + step) & (owners - 1))
                    tile = pl.ds(pl.multiple_of(at + chip * SLOTS, SLOTS), SLOTS)
                    old = buf_ref[tile, :].astype(F32)
                    new = jnp.where(iota((SLOTS, half), 0) == LABELS, label, old)
                    buf_ref[tile, :] = new.astype(BF)

            piece = pl.ds(at, rows)
            copy = pltpu.make_async_copy(
                buf_ref.at[piece], out_ref.at[piece], sem_ref.at[a * 2 + r]
            )
            copy.start()
            copies.append(copy)
    for copy in copies:
        copy.wait()


def prepare_kernel(
    wqk_ref, wv_ref, wo_ref, pos_ref, wq_ref, wvt_ref, wout_ref, slot_ref,
    wv_buf_ref, sem_ref, *, owners,
):
    width = wq_ref.shape[1]
    core = lax.axis_index("round")
    cols = pl.ds(pl.multiple_of(core * width, width), width)
    copies = [pltpu.make_async_copy(wo_ref, wout_ref, sem_ref.at[4])]
    for part in range(2):
        source = core + part - 2 * part * core
        rows = pl.ds(pl.multiple_of(source * width, width), width)
        there = pl.ds(part * width, width)
        copies += [
            pltpu.make_async_copy(wqk_ref.at[rows, cols], wq_ref.at[there], sem_ref.at[part]),
            pltpu.make_async_copy(wv_ref.at[rows, cols], wv_buf_ref.at[there], sem_ref.at[2 + part]),
        ]
    for copy in copies:
        copy.start()
    count = pos_ref.shape[1]
    for r in range(2):
        slot = slots_of(pos_ref[r : r + 1, :], owners)[1].astype(F32)
        slot_ref[r * count : (r + 1) * count, :] = jnp.transpose(
            jnp.broadcast_to(slot, (128, count))
        )
    for copy in copies:
        copy.wait()
    wvt_ref[...] = jnp.transpose(wv_buf_ref[...])


def meta_of(x_ref):
    rows = x_ref.shape[0]
    count = rows // SLOTS
    pick = mask(iota((count, rows), 1) == iota((count, rows), 0) * SLOTS + META)
    return mm(pick, x_ref[:, 0:128]).astype(BF)


def place_rows(meta):
    count = meta.shape[0]
    v, lane = iota((128, 128), 0), iota((128, 128), 1)
    j = lane & (SLOTS - 1)
    weight = jnp.where(v == 2 * j, 32.0, jnp.where(v == 2 * j + 1, 1.0, 0.0)).astype(BF)
    codes = mm(meta, weight)
    own = (iota((count, 128), 0) & 7) == (iota((count, 128), 1) >> 4)
    codes = jnp.where(own, codes, 0.0)
    return jnp.sum(codes.reshape(count // 8, 8, 128), axis=1)


def place_columns(meta):
    count = meta.shape[0]
    rows = count * SLOTS
    values = jnp.broadcast_to(meta.astype(F32)[:, None, :], (count, SLOTS, 128))
    keep = (iota((rows, 128), 1) >> 1) == (iota((rows, 128), 0) & (SLOTS - 1))
    values = jnp.where(keep, values.reshape(rows, 128), 0.0).astype(BF)
    weight = jnp.where((iota((128, 128), 0) & 1) == 0, 32.0, 1.0).astype(BF)
    return mm(values, weight)


def sorted_rows(x_ref, code_ref, out_refs, first):
    rows = sum(out_ref.shape[0] for out_ref in out_refs)
    position = (iota((rows, 128), 0) + (first + 32)).astype(F32)
    picks = [
        mask(position == jnp.broadcast_to(code_ref[q : q + 1, :], (rows, 128)))
        for q in range(code_ref.shape[0])
    ]
    result = mm(jnp.concatenate(picks, axis=1), x_ref[...]).astype(BF)
    at = 0
    for out_ref in out_refs:
        out_ref[...] = result[at : at + out_ref.shape[0]]
        at += out_ref.shape[0]


def sort_high_kernel(x_ref, high_ref, meta_ref, code_ref, wide_ref):
    meta = meta_of(x_ref)
    meta_ref[...] = meta
    lane = iota(meta.shape, 1)
    flags = jnp.where((lane >> 1) == SLOTS, meta.astype(F32), 0.0)
    flags = jnp.max(flags, axis=0, keepdims=True)
    wide_ref[...] = jnp.sum(flags, axis=1, keepdims=True)
    code_ref[...] = place_rows(meta)
    sorted_rows(x_ref, code_ref, (high_ref,), BLOCK - high_ref.shape[0])


def sort_low_kernel(
    x_ref, code_ref, low_ref, low_next_ref, row_ref, col_ref, prior_col_ref, flag_ref, *, owners
):
    my_round, me = lax.axis_index("head"), block_of(lax.axis_index("seq"))

    def labels(block):
        parts = []
        for half in range(2):
            source = (my_round * 2 + half) * owners + block
            rows = x_ref[pl.ds(pl.multiple_of(source * SLOTS, SLOTS), SLOTS), :].astype(F32)
            at_labels = iota(rows.shape, 0) == LABELS
            parts.append(jnp.sum(jnp.where(at_labels, rows, 0.0), axis=0, keepdims=True))
        return jnp.concatenate(parts, axis=1)

    own = labels(me)
    prior = labels((me + owners - 1) & (owners - 1))
    row_ref[...] = own
    col_ref[...] = jnp.transpose(jnp.broadcast_to(own, (TILE, BLOCK)))
    prior_col_ref[...] = jnp.transpose(jnp.broadcast_to(prior, (TILE, BLOCK)))
    flag_ref[...] = plan(own, prior)
    sorted_rows(x_ref, code_ref, (low_ref, low_next_ref), 0)


def window(i):
    return max(i * SPAN - TILE, 0), min((i + 1) * SPAN + TILE, BLOCK)


def plan(own, prior):
    first = prior[:, 0:1]

    def ends(labels):
        labels = jnp.where(labels < first, labels + SHIFT, labels)
        tiles = jnp.concatenate([labels[:, t : t + TILE] for t in range(0, BLOCK, TILE)], axis=0)
        low = jnp.min(tiles, axis=1, keepdims=True)
        high = jnp.max(tiles, axis=1, keepdims=True)
        return jnp.broadcast_to(low, tiles.shape), jnp.broadcast_to(high, tiles.shape)

    low, high = ends(own)
    prior_low, prior_high = ends(prior)
    tile = iota(low.shape, 0)
    weight = (1 << tile).astype(F32)
    per, tiles = SPAN // TILE, BLOCK // TILE

    def bits(found):
        return jnp.sum(jnp.where(found, weight, 0.0), axis=0, keepdims=True)

    words = []
    for i in range(SPANS):
        at = i * per
        span_low = jnp.min(low[at : at + per], axis=0, keepdims=True)
        span_high = jnp.max(high[at : at + per], axis=0, keepdims=True)
        begin, end = window(i)
        outside = (tile < begin // TILE) | (tile >= end // TILE)
        words.append(bits((low <= span_high) & (high >= span_low) & outside))
    some = jnp.zeros(low.shape, F32)
    late = jnp.zeros((1, TILE), F32)
    for i in range(tiles):
        meets = (prior_low <= high[i : i + 1]) & (prior_high >= low[i : i + 1])
        meets = jnp.where(meets, 1.0, 0.0)
        some = jnp.maximum(some, meets)
        late = late + float(2**i) * jnp.max(meets, axis=0, keepdims=True)
    some = jnp.where(tile < tiles - 1, some, 0.0)
    late = late + 256.0 * jnp.max(some, axis=0, keepdims=True)
    rows = [late, words[0] + 256.0 * words[1], words[2] + 256.0 * words[3]]
    return jnp.concatenate(rows + [jnp.zeros((5, TILE), F32)], axis=0)


def flag_bits(flag_ref, row):
    return jnp.max(flag_ref[row : row + 1, :]).astype(I32)


def project(mine, other, wq_ref, wvt_ref):
    width = mine.shape[1]
    queries = (mm(mine, wq_ref[0:width, :]) + mm(other, wq_ref[width:, :])).astype(BF)
    values = mm_nt(wvt_ref[:, 0:width], mine) + mm_nt(wvt_ref[:, width:], other)
    parts = []
    for h in range(queries.shape[1] // DH):
        rows = queries[:, head_cols(h)].astype(F32)
        sq = jnp.square(rows)
        top = sq.astype(BF)
        rest = (sq - top.astype(F32)).astype(BF)
        total = mm(jnp.concatenate([top, rest], axis=1), jnp.ones((2 * DH, 128), BF))
        keys = rows * (lax.rsqrt(total * (1.0 / DH) + EPSILON) * (LOG2E * DH ** (-0.5)))
        top = keys.astype(BF)
        parts += [top, (keys - top.astype(F32)).astype(BF)]
    return queries, parts, values.astype(BF)


def value_rows(h):
    return slice(h * (DH + 16), (h + 1) * (DH + 16))


def store_keys(at, parts, values, key_ref, vt_ref):
    rows = parts[0].shape[0]
    for h in range(len(parts) // 2):
        key_ref[at : at + rows, h * 2 * DH : h * 2 * DH + DH] = parts[2 * h]
        key_ref[at : at + rows, h * 2 * DH + DH : (h + 1) * 2 * DH] = parts[2 * h + 1]
        first = h * (DH + 16)
        vt_ref[first : first + DH, at : at + rows] = values[head_cols(h), :]
        vt_ref[first + DH : first + DH + 16, at : at + rows] = jnp.ones((16, rows), BF)


def score(keys, queries, key_label, query_label, diagonal):
    count, span = keys.shape[0], queries.shape[0]
    scores = mm_nt(keys, jnp.concatenate([queries, queries], axis=1))
    match = jnp.concatenate([key_label] * (span // TILE), axis=1) == query_label
    scores = jnp.where(match, scores, BUCKET_PENALTY)
    if isinstance(diagonal, int):
        cut = scores[diagonal : diagonal + span]
        cut = jnp.where(iota((span, span), 0) == iota((span, span), 1), SELF_PENALTY, cut)
        parts = [scores[:diagonal]] * (diagonal > 0) + [cut]
        parts += [scores[diagonal + span :]] * (diagonal + span < count)
        scores = jnp.concatenate(parts, axis=0) if len(parts) > 1 else cut
    elif diagonal is not None:
        apart = iota((count, span), 0) - iota((count, span), 1)
        scores = jnp.where(apart == diagonal, SELF_PENALTY, scores)
    return scores


def weigh(scores, values):
    top = jnp.max(scores, axis=0, keepdims=True)
    result = mm(values, jnp.exp2(scores - top).astype(BF))
    return result[0:DH], top, result[DH : DH + 1]


def merge_heads(keys, queries, values, key_label, query_label, at, out_ref, lse_ref):
    span = query_label.shape[1]
    lse_row = iota((8, span), 0)
    tiles = [lse_ref[:, pl.ds(at, span)]]

    def first(h):
        return score(keys(h), queries(h), key_label, query_label, None)

    def second(h, scores):
        result, top, total = weigh(scores, values(h))
        here, there = tiles[0][h : h + 1, :], top + jnp.log2(total)
        largest = jnp.maximum(here, there)
        kept, added = jnp.exp2(here - largest), jnp.exp2(there - largest)
        own = out_ref[head_cols(h), pl.ds(at, span)].astype(F32)
        merged = (kept * own + result * (added / total)) * (1.0 / (kept + added))
        out_ref[head_cols(h), pl.ds(at, span)] = merged.astype(BF)
        new = largest + jnp.log2(kept + added)
        tiles[0] = jnp.where(lse_row == h, new, tiles[0])

    ahead(range(out_ref.shape[0] // DH), first, second, 3)
    lse_ref[:, pl.ds(at, span)] = tiles[0]


def ahead(work, first, second, depth):
    pending = []
    for item in work:
        pending.append((item, first(item)))
        if len(pending) > depth:
            second(*pending.pop(0))
    for entry in pending:
        second(*entry)


def late_span(bits, i):
    return ((bits >> (SPAN // TILE * i)) & (2 ** (SPAN // TILE) - 1)) != 0


def sums_of(lse, heads):
    row = iota(lse.shape, 0)
    sums = jnp.zeros(lse.shape, F32)
    for h in range(heads):
        part = lse[h : h + 1, :]
        top = part.astype(BF).astype(F32)
        sums = jnp.where(row == 2 * h, top, jnp.where(row == 2 * h + 1, part - top, sums))
    return jnp.concatenate([sums] * SLOTS, axis=0).astype(BF)


def in_meta_row(sums):
    rows = sums.shape[0]
    row = iota((rows, 128), 0) & (SLOTS - 1)
    sums = jnp.where(row == (iota((rows, 128), 1) >> 3), sums, 0.0)
    sums = jnp.sum(sums.reshape(rows // SLOTS, SLOTS, 128), axis=1, keepdims=True)
    sums = jnp.broadcast_to(sums, (rows // SLOTS, SLOTS, 128)).reshape(rows, 128)
    return jnp.where(row == META, sums, 0.0)


def pick_of(codes, start, stop):
    lane = (iota(codes.shape, 1) + 32).astype(F32)
    return jnp.concatenate([mask(codes == lane + float(c)) for c in range(start, stop, 128)], 1)


def packed_rows(codes, out, sums):
    half = BLOCK // 2
    body = mm_nt(pick_of(codes, 0, BLOCK), out)
    upper = codes >= float(half + 32)
    both = jnp.concatenate([sums[:, :half], sums[:, half:]], axis=0)
    found = mm_nt(pick_of(jnp.where(upper, codes - half, codes), 0, half), both)
    extra = in_meta_row(jnp.where(upper, found[:, 128:], found[:, :128]))
    return jnp.concatenate([body[:, 0:128] + extra, body[:, 128:]], axis=1)


def first_kernel(hm_ref, ho_ref, wq_ref, wvt_ref, meta_ref, q_ref, key_ref, vt_ref, place_ref):
    queries, parts, values = project(hm_ref[...], ho_ref[...], wq_ref, wvt_ref)
    q_ref[...] = queries
    store_keys(0, parts, values, key_ref, vt_ref)
    place_ref[...] = place_columns(meta_ref[...])


def own_kernel(
    lm_ref, nm_ref, lo_ref, no_ref, q_high_ref, key_high_ref, vt_high_ref, wq_ref, wvt_ref,
    row_ref, col_ref, flag_ref, place_ref,
    q_ref, out_ref, lse_ref, early_ref, key_ref, vt_ref,
):
    low_rows = 2 * lm_ref.shape[0]
    heads = q_ref.shape[1] // DH
    late_bits = flag_bits(flag_ref, 0)
    far_bits = [flag_bits(flag_ref, 1), flag_bits(flag_ref, 2)]
    q_ref[low_rows:, :] = q_high_ref[...]
    key_ref[low_rows:, :] = key_high_ref[...]
    vt_ref[:, low_rows:] = vt_high_ref[...]
    mine = jnp.concatenate([lm_ref[...], nm_ref[...]], axis=0)
    other = jnp.concatenate([lo_ref[...], no_ref[...]], axis=0)
    queries, parts, values = project(mine, other, wq_ref, wvt_ref)
    q_ref[0:low_rows, :] = queries
    store_keys(0, parts, values, key_ref, vt_ref)
    lse_row = iota((8, SPAN), 0)

    def spans(work, depth):
        tiles = {}

        def first(item):
            h, at, start, size, diagonal = item
            return score(
                key_ref[pl.ds(start, size), head_cols(h, 2)], q_ref[pl.ds(at, SPAN), head_cols(h)],
                col_ref[pl.ds(start, size), :], row_ref[0:1, pl.ds(at, SPAN)], diagonal,
            )

        def second(item, scores):
            h, at, start, size, _ = item
            result, top, total = weigh(scores, vt_ref[value_rows(h), pl.ds(start, size)])
            out_ref[head_cols(h), pl.ds(at, SPAN)] = (result * (1.0 / total)).astype(BF)
            tile = tiles.pop("lse") if h else jnp.zeros((8, SPAN), F32)
            tiles["lse"] = jnp.where(lse_row == h, top + jnp.log2(total), tile)
            if h == heads - 1:
                lse_ref[:, pl.ds(at, SPAN)] = tiles.pop("lse")

        ahead(work, first, second, depth)

    work = []
    for at in range(BLOCK - SPAN, -1, -SPAN):
        start, stop = window(at // SPAN)
        work += [(h, at, start, stop - start, at - start) for h in range(heads)]
    spans(work, 3)

    for pair in range(2):

        @pl.when(far_bits[pair] != 0)
        def _():
            @pl.loop(0, 2 * BLOCK // TILE)
            def _(k):
                @pl.when(((far_bits[pair] >> k) & 1) != 0)
                def _():
                    at = pl.multiple_of((2 * pair + (k >> 3)) * SPAN, SPAN)
                    rows = pl.ds(pl.multiple_of((k & 7) * TILE, TILE), TILE)
                    merge_heads(
                        lambda h: key_ref[rows, head_cols(h, 2)],
                        lambda h: q_ref[pl.ds(at, SPAN), head_cols(h)],
                        lambda h: vt_ref[value_rows(h), rows],
                        col_ref[rows, :], row_ref[0:1, pl.ds(at, SPAN)], at, out_ref, lse_ref,
                    )

    sums = sums_of(lse_ref[...], heads)
    for at in range(0, early_ref.shape[0], STEP):
        codes = place_ref[at : at + STEP, :]
        for i in range(SPANS):
            late = jnp.where(late_span(late_bits, i), float(32 + i * SPAN), 4.0 * BLOCK)
            codes = jnp.where((codes >= late) & (codes < late + SPAN), 0.0, codes)
        early_ref[at : at + STEP, :] = packed_rows(codes, out_ref[...], sums).astype(BF)


def rest_kernel(
    xm_ref, xo_ref, wq_ref, wvt_ref, row_ref, col_ref, flag_ref,
    q_ref, own_ref, own_lse_ref, place_ref, early_ref, send_ref,
    out_ref, lse_ref, key_ref, vt_ref, buf_ref, sem_ref,
):
    halo = xm_ref.shape[0]
    heads = q_ref.shape[1] // DH
    bits = flag_bits(flag_ref, 0)
    lse_ref[...] = own_lse_ref[...]
    for i in range(SPANS):
        cols = slice(i * SPAN, (i + 1) * SPAN)

        @pl.when(late_span(bits, i))
        def _():
            out_ref[:, cols] = own_ref[:, cols]

        @pl.when(jnp.logical_not(late_span(bits, i)))
        def _():
            out_ref[:, cols] = jnp.zeros((heads * DH, SPAN), BF)
            lse_ref[:, cols] = jnp.zeros((8, SPAN), F32)

    def at_once(at, first, span):
        merge_heads(
            lambda h: key_ref[first:, head_cols(h, 2)],
            lambda h: q_ref[pl.ds(at, span), head_cols(h)],
            lambda h: vt_ref[value_rows(h), first:],
            col_ref[BLOCK - halo + first :, :], row_ref[0:1, pl.ds(at, span)], at, out_ref, lse_ref,
        )

    def merge(size):
        first = halo - size
        _, parts, values = project(xm_ref[first:, :], xo_ref[first:, :], wq_ref, wvt_ref)
        store_keys(first, parts, values, key_ref, vt_ref)
        many = 3 * TILE if size == 3 * TILE else TILE
        few = (bits & 255) < 2 ** (many // TILE)

        @pl.when(few & (bits != 0))
        def _():
            at_once(0, first, many)

        @pl.when(jnp.logical_not(few))
        def _():
            @pl.loop(0, BLOCK // TILE)
            def _(i):
                @pl.when(((bits >> i) & 1) != 0)
                def _():
                    at_once(pl.multiple_of(i * TILE, TILE), first, TILE)

    if halo > HALO:
        merge(halo)
    else:
        pl.when(bits < 256)(lambda: merge(TILE))
        pl.when(bits >= 256)(lambda: merge(halo))

    pieces = send_ref.shape[0] // PIECE

    def sending(t):
        piece = pl.ds(pl.multiple_of(t * PIECE, PIECE), PIECE)
        return pltpu.make_async_copy(buf_ref.at[piece], send_ref.at[piece], sem_ref.at[t])

    def complete(piece, codes, rows_ref, cols):
        pick = pick_of(codes, 0, cols.size)
        body = mm_nt(pick, out_ref[:, cols])
        extra = in_meta_row(mm_nt(pick, sums_of(lse_ref[:, cols], heads)))
        rows = jnp.concatenate([body[:, 0:128] + extra, body[:, 128:]], axis=1)
        buf_ref[piece, :] = (rows_ref[piece, :].astype(F32) + rows).astype(BF)

    def finish(span):
        @pl.loop(0, pieces)
        def _(t):
            piece = pl.ds(pl.multiple_of(t * PIECE, PIECE), PIECE)
            complete(piece, place_ref[piece, :], early_ref, pl.ds(0, span))
            sending(t).start()

    needed = bits & 255
    pl.when(needed < 2 ** (SPAN // TILE))(lambda: finish(SPAN))
    pl.when((needed >= 2 ** (SPAN // TILE)) & (needed < 2 ** (2 * SPAN // TILE)))(
        lambda: finish(2 * SPAN)
    )

    @pl.when(needed >= 2 ** (2 * SPAN // TILE))
    def _():
        @pl.loop(0, pieces)
        def _(t):
            piece = pl.ds(pl.multiple_of(t * PIECE, PIECE), PIECE)
            buf_ref[piece, :] = early_ref[piece, :]

            @pl.loop(0, SPANS)
            def _(i):
                @pl.when(late_span(bits, i))
                def _():
                    codes = place_ref[piece, :] - (i * SPAN).astype(F32)
                    cols = pl.ds(pl.multiple_of(i * SPAN, SPAN), SPAN)
                    complete(piece, codes, buf_ref, cols)

            sending(t).start()

    @pl.loop(0, pieces)
    def _(t):
        sending(t).wait()


def final_kernel(x_ref, slot_ref, w_ref, out_ref, *, owners):
    count = out_ref.shape[0]
    width = x_ref.shape[1]
    rows = owners * SLOTS
    lane = iota((count, 128), 1)
    picks, meta_picks, ranks = [], [], []
    for r in range(2):
        slot = slot_ref[r * count : (r + 1) * count, :].astype(I32)
        place = slot & (SLOTS - 1)
        at_meta = slot - place + META
        picks.append(
            jnp.concatenate([mask(slot == lane + c) for c in range(0, rows, 128)], axis=1)
        )
        meta_picks.append(
            jnp.concatenate([mask(at_meta == lane + c) for c in range(0, rows, 128)], axis=1)
        )
        ranks.append(place)
    sums = []
    for r in range(2):
        there = [x_ref[(a * 2 + r) * rows : (a * 2 + r + 1) * rows, 0:128] for a in range(2)]
        own = mm(meta_picks[r], jnp.concatenate(there, axis=1))
        keep = (lane >> 3) == ranks[r]
        sums.append([jnp.where(keep, own[:, a * 128 : (a + 1) * 128], 0.0) for a in range(2)])
    v = iota((256, width), 0)
    select = jnp.where(((v & 7) >> 1) == (iota((256, width), 1) >> 7), 1.0, 0.0)
    select = jnp.where(v < 128, -select, select).astype(BF)
    total = None
    for a in range(2):
        values = [
            mm(picks[r], x_ref[(a * 2 + r) * rows : (a * 2 + r + 1) * rows, :]) for r in range(2)
        ]
        apart = mm(jnp.concatenate([sums[0][a], sums[1][a]], axis=1).astype(BF), select)
        small = jnp.exp2(-jnp.abs(apart))
        large = 1.0 / (1.0 + small)
        second = jnp.where(apart < 0.0, small * large, large)
        first = jnp.where(apart < 0.0, large, small * large)
        combined = (first * values[0] + second * values[1]).astype(BF)
        part = mm(combined, w_ref[a * width : (a + 1) * width, :])
        total = part if total is None else total + part
    out_ref[...] = total.astype(BF)


def shards(tokens, w_qk, w_v, w_out, positions, buckets):
    tok_dev, model_width = tokens.shape
    owners = lax.axis_size("seq")
    total = 2 * 2 * owners
    width = model_width // 2
    heads = width // DH
    rows = total * SLOTS
    params = pltpu.CompilerParams(vmem_limit_bytes=24 * 2**20)
    alone = pltpu.CompilerParams(vmem_limit_bytes=60 * 2**20)
    in_vmem = pl.BlockSpec(memory_space=pltpu.VMEM)
    in_hbm = pl.BlockSpec(memory_space=pltpu.HBM)

    def shape(*dims, dtype=BF):
        return jax.ShapeDtypeStruct(dims, dtype)

    def cost(flops, moved):
        return pl.CostEstimate(flops=flops, bytes_accessed=moved, transcendentals=0)

    def swap(x):
        return lax.ppermute(x, "round", [(0, 1), (1, 0)])

    def onward(x):
        route = [(chip_of(i), chip_of((i + 1) % owners)) for i in range(owners)]
        return lax.ppermute(x, "seq", route)

    def exchange(x):
        x = x.reshape(total, SLOTS, width)
        x = lax.all_to_all(x, AXES, split_axis=0, concat_axis=0, tiled=True)
        return x.reshape(rows, width)

    packed = pl.pallas_call(
        functools.partial(pack_kernel, owners=owners),
        out_shape=shape(rows, width),
        in_specs=[in_hbm, in_vmem, in_vmem],
        out_specs=in_hbm,
        scratch_shapes=[
            pltpu.VMEM((tok_dev, model_width), BF),
            pltpu.VMEM((rows, width), BF),
            pltpu.SemaphoreType.DMA((2,)),
            pltpu.SemaphoreType.DMA((4,)),
        ],
        compiler_params=alone,
        name="pack",
    )(tokens, positions, buckets)
    arrived = exchange(packed)

    wq, wvt, wout, slots = pl.pallas_call(
        functools.partial(prepare_kernel, owners=owners),
        out_shape=[
            shape(model_width, width),
            shape(width, model_width),
            shape(model_width, model_width),
            shape(2 * tok_dev, 128, dtype=F32),
        ],
        in_specs=[in_hbm] * 3 + [in_vmem],
        out_specs=[in_vmem] * 4,
        scratch_shapes=[pltpu.VMEM((model_width, width), BF), pltpu.SemaphoreType.DMA((5,))],
        compiler_params=params,
        cost_estimate=cost(2**30, 8 * 2**20),
        name="prepare",
    )(w_qk, w_v, w_out, positions)
    arrived, wq, wvt, wout, slots = lax.optimization_barrier((arrived, wq, wvt, wout, slots))

    high, meta, codes, wide = pl.pallas_call(
        sort_high_kernel,
        out_shape=[
            shape(HALO, width),
            shape(total, 128),
            shape(total // 8, 128, dtype=F32),
            shape(1, 1, dtype=F32),
        ],
        compiler_params=params,
        name="sort_high",
    )(arrived)
    halo = onward(high)
    high_other = swap(high)
    low, low_next, label_row, label_col, prior_col, flags = pl.pallas_call(
        functools.partial(sort_low_kernel, owners=owners),
        out_shape=[
            shape((BLOCK - HALO) // 2, width),
            shape((BLOCK - HALO) // 2, width),
            shape(1, BLOCK, dtype=F32),
            shape(BLOCK, TILE, dtype=F32),
            shape(BLOCK, TILE, dtype=F32),
            shape(8, 128, dtype=F32),
        ],
        compiler_params=params,
        cost_estimate=cost(4 * BLOCK * rows * width, 4 * 2**20),
        name="sort_low",
    )(arrived, codes)
    low_other, low_next_other = swap(low), swap(low_next)

    values_shape = (heads * (DH + 16), BLOCK)
    q_high, key_high, vt_high, places = pl.pallas_call(
        first_kernel,
        out_shape=[
            shape(HALO, width),
            shape(HALO, 2 * width),
            shape(values_shape[0], HALO),
            shape(rows, 128, dtype=F32),
        ],
        compiler_params=params,
        cost_estimate=cost(4 * HALO * model_width * width, 2**20),
        name="own_rows",
    )(high, high_other, wq, wvt, meta)
    queries, own_out, own_lse, early = pl.pallas_call(
        own_kernel,
        out_shape=[
            shape(BLOCK, width),
            shape(width, BLOCK),
            shape(8, BLOCK, dtype=F32),
            shape(rows, width),
        ],
        scratch_shapes=[pltpu.VMEM((BLOCK, 2 * width), BF), pltpu.VMEM(values_shape, BF)],
        compiler_params=params,
        cost_estimate=cost(2**20, 2**20),
        name="own_block",
    )(
        low, low_next, low_other, low_next_other, q_high, key_high, vt_high, wq, wvt,
        label_row, label_col, flags, places,
    )
    halo, own_lse = lax.optimization_barrier((halo, own_lse))

    def finish(halo_mine, halo_other):
        size = halo_mine.shape[0]
        return pl.pallas_call(
            rest_kernel,
            out_shape=shape(rows, width),
            in_specs=[in_vmem] * 12,
            out_specs=in_hbm,
            scratch_shapes=[
                pltpu.VMEM((width, BLOCK), BF),
                pltpu.VMEM((8, BLOCK), F32),
                pltpu.VMEM((size, 2 * width), BF),
                pltpu.VMEM((heads * (DH + 16), size), BF),
                pltpu.VMEM((rows, width), BF),
                pltpu.SemaphoreType.DMA((rows // PIECE,)),
            ],
            compiler_params=params,
            name="prior_block",
        )(
            halo_mine, halo_other, wq, wvt, label_row, prior_col, flags,
            queries, own_out, own_lse, places, early,
        )

    halo_other = swap(halo)

    def more(rows):
        rest = onward(rows)
        return finish(
            jnp.concatenate([rest, halo], axis=0),
            jnp.concatenate([swap(rest), halo_other], axis=0),
        )

    back = lax.cond(wide[0, 0] > 0.0, lambda: more(jnp.concatenate([low, low_next], axis=0)), lambda: finish(halo, halo_other))
    returned = exchange(back)
    return pl.pallas_call(
        functools.partial(final_kernel, owners=owners),
        out_shape=shape(tok_dev, model_width),
        compiler_params=params,
        name="combine",
    )(returned, slots, wout)


def solution(mesh):
    in_specs = (
        P(("round", "head", "seq"), None),
        P(),
        P(),
        P(),
        P(None, ("round", "head", "seq")),
        P("round", "seq"),
    )
    out_specs = P(("round", "head", "seq"), None)
    return jax.shard_map(shards, mesh=mesh, in_specs=in_specs, out_specs=out_specs, check_vma=False)
```

```python
import functools

import jax
import jax.numpy as jnp
from jax import lax
from jax.experimental import pallas as pl
from jax.experimental.pallas import tpu as pltpu
from jax.sharding import PartitionSpec as P

DH = 128
BLOCK = 1024
TILE = 128
SPAN = 256
SPANS = BLOCK // SPAN
SLOTS = 16
META = 14
LABELS = 15
HALO = 3 * TILE
SHIFT = 65536.0
STEP = 1024
PIECE = 512

LOG2E = 1.4426950408889634
SELF_PENALTY = -100000.0 * LOG2E
BUCKET_PENALTY = -1000000000.0
EPSILON = 1e-06

BF = jnp.bfloat16
F32 = jnp.float32
I32 = jnp.int32
NT = (((1,), (1,)), ((), ()))
AXES = ("round", "head", "seq")


def iota(shape, dim):
    return lax.broadcasted_iota(I32, shape, dim)


def mask(cond):
    return jnp.where(cond, 1.0, 0.0).astype(BF)


def mm(a, b):
    return jnp.dot(a, b, preferred_element_type=F32)


def mm_nt(a, b):
    return lax.dot_general(a, b, NT, preferred_element_type=F32)


def head_cols(h, wide=1):
    return slice(h * DH * wide, (h + 1) * DH * wide)


def chip_of(block):
    y = block >> 3
    ring = (block & 7) ^ ((y & 1) * 7)
    return (y << 3) | (ring & 4) | ((ring & 3) ^ ((ring >> 2) * 3))


def block_of(chip):
    y = chip >> 3
    x = (chip >> 2) & 1
    ring = (x << 2) | ((chip & 3) ^ (x * 3))
    return (y << 3) | (ring ^ ((y & 1) * 7))


def slots_of(pos, owners):
    count = pos.shape[1]
    dest = chip_of(pos >> 10)
    hot = iota((owners, count), 0) == dest
    earlier = mask(iota((count, count), 0) < iota((count, count), 1))
    before = mm(mask(hot), earlier)
    rank = jnp.sum(jnp.where(hot, before, 0.0), axis=0, keepdims=True).astype(I32)
    return hot, dest * SLOTS + rank


def pack_kernel(
    tok_hbm_ref, pos_hbm_ref, label_hbm_ref, out_ref,
    tok_ref, pos_ref, label_ref, buf_ref, in_sem, sem_ref, *, owners,
):
    count = tok_ref.shape[0]
    width = out_ref.shape[1]
    rows = owners * SLOTS
    half = BLOCK // 2
    small = [
        pltpu.make_async_copy(pos_hbm_ref, pos_ref, in_sem.at[2]),
        pltpu.make_async_copy(label_hbm_ref, label_ref, in_sem.at[3]),
    ]
    loads = []
    for a in range(2):
        cols = pl.ds(a * width, width)
        loads.append(
            pltpu.make_async_copy(tok_hbm_ref.at[:, cols], tok_ref.at[:, cols], in_sem.at[a])
        )
    for load in small + loads:
        load.start()
    for load in small:
        load.wait()
    first, last = label_ref[0:1, 0:1], label_ref[0:1, BLOCK - 1 : BLOCK]
    wide = []
    for held in (HALO, half):
        middle = label_ref[0:1, BLOCK - held - 1 : BLOCK - held]
        marked = jnp.where(last == 0, jnp.minimum(first, middle), jnp.abs(middle - last))
        wide.append(jnp.where(jnp.broadcast_to(marked, (owners, 128)) == 0, 1.0, 0.0))
    label = label_ref[...]
    label = ((128 + (label & 127)) << (label >> 7)).astype(F32)
    core, head, seq = (lax.axis_index(axis) for axis in AXES)
    label = jnp.where(head == 0, label[:, :half], label[:, half:])
    label = jnp.broadcast_to(label, (SLOTS, half))
    copies = []
    for r in range(2):
        pos = pos_ref[r : r + 1, :]
        hot, slot = slots_of(pos, owners)
        rank = slot & (SLOTS - 1)
        within = pos & (BLOCK - 1)
        pick = mask(iota((rows, count), 0) == slot)
        value = iota((128, count), 0)
        code = jnp.where((value & 1) == 0, (within >> 5) + 1, within & 31)
        code = jnp.where((value >> 1) == rank, code, 0).astype(F32).astype(BF)
        places = mm_nt(mask(hot), code)
        lane = iota((owners, 128), 1)
        places = jnp.where(lane == 2 * SLOTS, wide[0], places)
        places = jnp.where(lane == 2 * SLOTS + 1, wide[1], places).astype(BF)
        at_meta = mask(iota((rows, owners), 0) == iota((rows, owners), 1) * SLOTS + META)
        extra = mm(at_meta, places)
        for a in range(2):
            if r == 0:
                loads[a].wait()
            at = (a * 2 + r) * rows
            body = mm(pick, tok_ref[:, a * width : (a + 1) * width])
            buf_ref[at : at + rows, 0:128] = (body[:, 0:128] + extra).astype(BF)
            buf_ref[at : at + rows, 128:width] = body[:, 128:].astype(BF)

            @pl.when(core == r)
            def _():
                for step in range(2):
                    chip = chip_of((seq + step) & (owners - 1))
                    tile = pl.ds(pl.multiple_of(at + chip * SLOTS, SLOTS), SLOTS)
                    old = buf_ref[tile, :].astype(F32)
                    new = jnp.where(iota((SLOTS, half), 0) == LABELS, label, old)
                    buf_ref[tile, :] = new.astype(BF)

            piece = pl.ds(at, rows)
            copy = pltpu.make_async_copy(
                buf_ref.at[piece], out_ref.at[piece], sem_ref.at[a * 2 + r]
            )
            copy.start()
            copies.append(copy)
    for copy in copies:
        copy.wait()


def prepare_kernel(
    wqk_ref, wv_ref, wo_ref, pos_ref, wq_ref, wvt_ref, wout_ref, slot_ref,
    wv_buf_ref, sem_ref, *, owners,
):
    width = wq_ref.shape[1]
    core = lax.axis_index("round")
    cols = pl.ds(pl.multiple_of(core * width, width), width)
    copies = [pltpu.make_async_copy(wo_ref, wout_ref, sem_ref.at[4])]
    for part in range(2):
        source = core + part - 2 * part * core
        rows = pl.ds(pl.multiple_of(source * width, width), width)
        there = pl.ds(part * width, width)
        copies += [
            pltpu.make_async_copy(wqk_ref.at[rows, cols], wq_ref.at[there], sem_ref.at[part]),
            pltpu.make_async_copy(wv_ref.at[rows, cols], wv_buf_ref.at[there], sem_ref.at[2 + part]),
        ]
    for copy in copies:
        copy.start()
    count = pos_ref.shape[1]
    for r in range(2):
        slot = slots_of(pos_ref[r : r + 1, :], owners)[1].astype(F32)
        slot_ref[r * count : (r + 1) * count, :] = jnp.transpose(
            jnp.broadcast_to(slot, (128, count))
        )
    for copy in copies:
        copy.wait()
    wvt_ref[...] = jnp.transpose(wv_buf_ref[...])


def meta_of(x_ref):
    rows = x_ref.shape[0]
    count = rows // SLOTS
    pick = mask(iota((count, rows), 1) == iota((count, rows), 0) * SLOTS + META)
    return mm(pick, x_ref[:, 0:128]).astype(BF)


def place_rows(meta):
    count = meta.shape[0]
    v, lane = iota((128, 128), 0), iota((128, 128), 1)
    j = lane & (SLOTS - 1)
    weight = jnp.where(v == 2 * j, 32.0, jnp.where(v == 2 * j + 1, 1.0, 0.0)).astype(BF)
    codes = mm(meta, weight)
    own = (iota((count, 128), 0) & 7) == (iota((count, 128), 1) >> 4)
    codes = jnp.where(own, codes, 0.0)
    return jnp.sum(codes.reshape(count // 8, 8, 128), axis=1)


def place_columns(meta):
    count = meta.shape[0]
    rows = count * SLOTS
    values = jnp.broadcast_to(meta.astype(F32)[:, None, :], (count, SLOTS, 128))
    keep = (iota((rows, 128), 1) >> 1) == (iota((rows, 128), 0) & (SLOTS - 1))
    values = jnp.where(keep, values.reshape(rows, 128), 0.0).astype(BF)
    weight = jnp.where((iota((128, 128), 0) & 1) == 0, 32.0, 1.0).astype(BF)
    return mm(values, weight)


def sorted_rows(x_ref, code_ref, out_refs, first):
    rows = sum(out_ref.shape[0] for out_ref in out_refs)
    position = (iota((rows, 128), 0) + (first + 32)).astype(F32)
    picks = [
        mask(position == jnp.broadcast_to(code_ref[q : q + 1, :], (rows, 128)))
        for q in range(code_ref.shape[0])
    ]
    result = mm(jnp.concatenate(picks, axis=1), x_ref[...]).astype(BF)
    at = 0
    for out_ref in out_refs:
        out_ref[...] = result[at : at + out_ref.shape[0]]
        at += out_ref.shape[0]


def sort_high_kernel(x_ref, high_ref, meta_ref, code_ref, wide_ref):
    meta = meta_of(x_ref)
    meta_ref[...] = meta
    lane = iota(meta.shape, 1)
    flags = jnp.where((lane >> 1) == SLOTS, meta.astype(F32), 0.0)
    flags = jnp.max(flags, axis=0, keepdims=True)
    wide_ref[...] = jnp.sum(flags, axis=1, keepdims=True)
    code_ref[...] = place_rows(meta)
    sorted_rows(x_ref, code_ref, (high_ref,), BLOCK - high_ref.shape[0])


def sort_low_kernel(
    x_ref, code_ref, low_ref, low_next_ref, row_ref, col_ref, prior_col_ref, flag_ref, *, owners
):
    my_round, me = lax.axis_index("head"), block_of(lax.axis_index("seq"))

    def labels(block):
        parts = []
        for half in range(2):
            source = (my_round * 2 + half) * owners + block
            rows = x_ref[pl.ds(pl.multiple_of(source * SLOTS, SLOTS), SLOTS), :].astype(F32)
            at_labels = iota(rows.shape, 0) == LABELS
            parts.append(jnp.sum(jnp.where(at_labels, rows, 0.0), axis=0, keepdims=True))
        return jnp.concatenate(parts, axis=1)

    own = labels(me)
    prior = labels((me + owners - 1) & (owners - 1))
    row_ref[...] = own
    col_ref[...] = jnp.transpose(jnp.broadcast_to(own, (TILE, BLOCK)))
    prior_col_ref[...] = jnp.transpose(jnp.broadcast_to(prior, (TILE, BLOCK)))
    flag_ref[...] = plan(own, prior)
    sorted_rows(x_ref, code_ref, (low_ref, low_next_ref), 0)


def window(i):
    start = i * SPAN - TILE * (1 + (i == 1))
    stop = (i + 1) * SPAN + TILE * (1 + (i == SPANS - 2))
    return max(start, 0), min(stop, BLOCK)


def plan(own, prior):
    first = prior[:, 0:1]

    def ends(labels):
        labels = jnp.where(labels < first, labels + SHIFT, labels)
        tiles = jnp.concatenate([labels[:, t : t + TILE] for t in range(0, BLOCK, TILE)], axis=0)
        low = jnp.min(tiles, axis=1, keepdims=True)
        high = jnp.max(tiles, axis=1, keepdims=True)
        return jnp.broadcast_to(low, tiles.shape), jnp.broadcast_to(high, tiles.shape)

    low, high = ends(own)
    prior_low, prior_high = ends(prior)
    tile = iota(low.shape, 0)
    weight = (1 << tile).astype(F32)
    per, tiles = SPAN // TILE, BLOCK // TILE

    def bits(found):
        return jnp.sum(jnp.where(found, weight, 0.0), axis=0, keepdims=True)

    words = []
    for i in range(SPANS):
        at = i * per
        span_low = jnp.min(low[at : at + per], axis=0, keepdims=True)
        span_high = jnp.max(high[at : at + per], axis=0, keepdims=True)
        begin, end = window(i)
        outside = (tile < begin // TILE) | (tile >= end // TILE)
        words.append(bits((low <= span_high) & (high >= span_low) & outside))
    some = jnp.zeros(low.shape, F32)
    late = jnp.zeros((1, TILE), F32)
    for i in range(tiles):
        meets = (prior_low <= high[i : i + 1]) & (prior_high >= low[i : i + 1])
        meets = jnp.where(meets, 1.0, 0.0)
        some = jnp.maximum(some, meets)
        late = late + float(2**i) * jnp.max(meets, axis=0, keepdims=True)
    some = jnp.where(tile < tiles - 1, some, 0.0)
    late = late + 256.0 * jnp.max(some, axis=0, keepdims=True)
    rows = [late, words[0] + 256.0 * words[1], words[2] + 256.0 * words[3]]
    return jnp.concatenate(rows + [jnp.zeros((5, TILE), F32)], axis=0)


def flag_bits(flag_ref, row):
    return jnp.max(flag_ref[row : row + 1, :]).astype(I32)


def project(mine, other, wq_ref, wvt_ref):
    width = mine.shape[1]
    queries = (mm(mine, wq_ref[0:width, :]) + mm(other, wq_ref[width:, :])).astype(BF)
    values = mm_nt(wvt_ref[:, 0:width], mine) + mm_nt(wvt_ref[:, width:], other)
    parts = []
    for h in range(queries.shape[1] // DH):
        rows = queries[:, head_cols(h)].astype(F32)
        sq = jnp.square(rows)
        top = sq.astype(BF)
        rest = (sq - top.astype(F32)).astype(BF)
        total = mm(jnp.concatenate([top, rest], axis=1), jnp.ones((2 * DH, 128), BF))
        keys = rows * (lax.rsqrt(total * (1.0 / DH) + EPSILON) * (LOG2E * DH ** (-0.5)))
        top = keys.astype(BF)
        parts += [top, (keys - top.astype(F32)).astype(BF)]
    return queries, parts, values.astype(BF)


def value_rows(h):
    return slice(h * (DH + 16), (h + 1) * (DH + 16))


def store_keys(at, parts, values, key_ref, vt_ref):
    rows = parts[0].shape[0]
    for h in range(len(parts) // 2):
        key_ref[at : at + rows, h * 2 * DH : h * 2 * DH + DH] = parts[2 * h]
        key_ref[at : at + rows, h * 2 * DH + DH : (h + 1) * 2 * DH] = parts[2 * h + 1]
        first = h * (DH + 16)
        vt_ref[first : first + DH, at : at + rows] = values[head_cols(h), :]
        vt_ref[first + DH : first + DH + 16, at : at + rows] = jnp.ones((16, rows), BF)


def score(keys, queries, key_label, query_label, diagonal):
    count, span = keys.shape[0], queries.shape[0]
    scores = mm_nt(keys, jnp.concatenate([queries, queries], axis=1))
    match = jnp.concatenate([key_label] * (span // TILE), axis=1) == query_label
    scores = jnp.where(match, scores, BUCKET_PENALTY)
    if isinstance(diagonal, int):
        cut = scores[diagonal : diagonal + span]
        cut = jnp.where(iota((span, span), 0) == iota((span, span), 1), SELF_PENALTY, cut)
        parts = [scores[:diagonal]] * (diagonal > 0) + [cut]
        parts += [scores[diagonal + span :]] * (diagonal + span < count)
        scores = jnp.concatenate(parts, axis=0) if len(parts) > 1 else cut
    elif diagonal is not None:
        apart = iota((count, span), 0) - iota((count, span), 1)
        scores = jnp.where(apart == diagonal, SELF_PENALTY, scores)
    return scores


def weigh(scores, values):
    top = jnp.max(scores, axis=0, keepdims=True)
    result = mm(values, jnp.exp2(scores - top).astype(BF))
    return result[0:DH], top, result[DH : DH + 1]


def merge_heads(keys, queries, values, key_label, query_label, at, out_ref, lse_ref):
    span = query_label.shape[1]
    lse_row = iota((8, span), 0)
    tiles = [lse_ref[:, pl.ds(at, span)]]

    def first(h):
        return score(keys(h), queries(h), key_label, query_label, None)

    def second(h, scores):
        result, top, total = weigh(scores, values(h))
        here, there = tiles[0][h : h + 1, :], top + jnp.log2(total)
        largest = jnp.maximum(here, there)
        kept, added = jnp.exp2(here - largest), jnp.exp2(there - largest)
        own = out_ref[head_cols(h), pl.ds(at, span)].astype(F32)
        merged = (kept * own + result * (added / total)) * (1.0 / (kept + added))
        out_ref[head_cols(h), pl.ds(at, span)] = merged.astype(BF)
        new = largest + jnp.log2(kept + added)
        tiles[0] = jnp.where(lse_row == h, new, tiles[0])

    ahead(range(out_ref.shape[0] // DH), first, second, 3)
    lse_ref[:, pl.ds(at, span)] = tiles[0]


def ahead(work, first, second, depth):
    pending = []
    for item in work:
        pending.append((item, first(item)))
        if len(pending) > depth:
            second(*pending.pop(0))
    for entry in pending:
        second(*entry)


def late_span(bits, i):
    return ((bits >> (SPAN // TILE * i)) & (2 ** (SPAN // TILE) - 1)) != 0


def sums_of(lse, heads):
    row = iota(lse.shape, 0)
    sums = jnp.zeros(lse.shape, F32)
    for h in range(heads):
        part = lse[h : h + 1, :]
        top = part.astype(BF).astype(F32)
        sums = jnp.where(row == 2 * h, top, jnp.where(row == 2 * h + 1, part - top, sums))
    return jnp.concatenate([sums] * SLOTS, axis=0).astype(BF)


def in_meta_row(sums):
    rows = sums.shape[0]
    row = iota((rows, 128), 0) & (SLOTS - 1)
    sums = jnp.where(row == (iota((rows, 128), 1) >> 3), sums, 0.0)
    sums = jnp.sum(sums.reshape(rows // SLOTS, SLOTS, 128), axis=1, keepdims=True)
    sums = jnp.broadcast_to(sums, (rows // SLOTS, SLOTS, 128)).reshape(rows, 128)
    return jnp.where(row == META, sums, 0.0)


def pick_of(codes, start, stop):
    lane = (iota(codes.shape, 1) + 32).astype(F32)
    return jnp.concatenate([mask(codes == lane + float(c)) for c in range(start, stop, 128)], 1)


def packed_rows(codes, out, sums):
    half = BLOCK // 2
    body = mm_nt(pick_of(codes, 0, BLOCK), out)
    upper = codes >= float(half + 32)
    both = jnp.concatenate([sums[:, :half], sums[:, half:]], axis=0)
    found = mm_nt(pick_of(jnp.where(upper, codes - half, codes), 0, half), both)
    extra = in_meta_row(jnp.where(upper, found[:, 128:], found[:, :128]))
    return jnp.concatenate([body[:, 0:128] + extra, body[:, 128:]], axis=1)


def first_kernel(hm_ref, ho_ref, wq_ref, wvt_ref, meta_ref, q_ref, key_ref, vt_ref, place_ref):
    queries, parts, values = project(hm_ref[...], ho_ref[...], wq_ref, wvt_ref)
    q_ref[...] = queries
    store_keys(0, parts, values, key_ref, vt_ref)
    place_ref[...] = place_columns(meta_ref[...])


def own_kernel(
    lm_ref, nm_ref, lo_ref, no_ref, q_high_ref, key_high_ref, vt_high_ref, wq_ref, wvt_ref,
    row_ref, col_ref, flag_ref, place_ref,
    q_ref, out_ref, lse_ref, early_ref, key_ref, vt_ref,
):
    low_rows = 2 * lm_ref.shape[0]
    heads = q_ref.shape[1] // DH
    late_bits = flag_bits(flag_ref, 0)
    far_bits = [flag_bits(flag_ref, 1), flag_bits(flag_ref, 2)]
    q_ref[low_rows:, :] = q_high_ref[...]
    key_ref[low_rows:, :] = key_high_ref[...]
    vt_ref[:, low_rows:] = vt_high_ref[...]
    mine = jnp.concatenate([lm_ref[...], nm_ref[...]], axis=0)
    other = jnp.concatenate([lo_ref[...], no_ref[...]], axis=0)
    queries, parts, values = project(mine, other, wq_ref, wvt_ref)
    q_ref[0:low_rows, :] = queries
    store_keys(0, parts, values, key_ref, vt_ref)
    lse_row = iota((8, SPAN), 0)

    def spans(work, depth):
        tiles = {}

        def first(item):
            h, at, start, size, diagonal = item
            return score(
                key_ref[pl.ds(start, size), head_cols(h, 2)], q_ref[pl.ds(at, SPAN), head_cols(h)],
                col_ref[pl.ds(start, size), :], row_ref[0:1, pl.ds(at, SPAN)], diagonal,
            )

        def second(item, scores):
            h, at, start, size, _ = item
            result, top, total = weigh(scores, vt_ref[value_rows(h), pl.ds(start, size)])
            out_ref[head_cols(h), pl.ds(at, SPAN)] = (result * (1.0 / total)).astype(BF)
            tile = tiles.pop("lse") if h else jnp.zeros((8, SPAN), F32)
            tiles["lse"] = jnp.where(lse_row == h, top + jnp.log2(total), tile)
            if h == heads - 1:
                lse_ref[:, pl.ds(at, SPAN)] = tiles.pop("lse")

        ahead(work, first, second, depth)

    work = []
    for at in range(BLOCK - SPAN, -1, -SPAN):
        start, stop = window(at // SPAN)
        work += [(h, at, start, stop - start, at - start) for h in range(heads)]
    spans(work, 3)

    for pair in range(2):

        @pl.when(far_bits[pair] != 0)
        def _():
            @pl.loop(0, 2 * BLOCK // TILE)
            def _(k):
                @pl.when(((far_bits[pair] >> k) & 1) != 0)
                def _():
                    at = pl.multiple_of((2 * pair + (k >> 3)) * SPAN, SPAN)
                    rows = pl.ds(pl.multiple_of((k & 7) * TILE, TILE), TILE)
                    merge_heads(
                        lambda h: key_ref[rows, head_cols(h, 2)],
                        lambda h: q_ref[pl.ds(at, SPAN), head_cols(h)],
                        lambda h: vt_ref[value_rows(h), rows],
                        col_ref[rows, :], row_ref[0:1, pl.ds(at, SPAN)], at, out_ref, lse_ref,
                    )

    sums = sums_of(lse_ref[...], heads)
    for at in range(0, early_ref.shape[0], STEP):
        codes = place_ref[at : at + STEP, :]
        for i in range(SPANS):
            late = jnp.where(late_span(late_bits, i), float(32 + i * SPAN), 4.0 * BLOCK)
            codes = jnp.where((codes >= late) & (codes < late + SPAN), 0.0, codes)
        early_ref[at : at + STEP, :] = packed_rows(codes, out_ref[...], sums).astype(BF)


def rest_kernel(
    xm_ref, xo_ref, wq_ref, wvt_ref, row_ref, col_ref, flag_ref,
    q_ref, own_ref, own_lse_ref, place_ref, early_ref, send_ref,
    out_ref, lse_ref, key_ref, vt_ref, buf_ref, sem_ref,
):
    halo = xm_ref.shape[0]
    heads = q_ref.shape[1] // DH
    bits = flag_bits(flag_ref, 0)
    lse_ref[...] = own_lse_ref[...]
    for i in range(SPANS):
        cols = slice(i * SPAN, (i + 1) * SPAN)

        @pl.when(late_span(bits, i))
        def _():
            out_ref[:, cols] = own_ref[:, cols]

        @pl.when(jnp.logical_not(late_span(bits, i)))
        def _():
            out_ref[:, cols] = jnp.zeros((heads * DH, SPAN), BF)
            lse_ref[:, cols] = jnp.zeros((8, SPAN), F32)

    def at_once(at, first, span):
        merge_heads(
            lambda h: key_ref[first:, head_cols(h, 2)],
            lambda h: q_ref[pl.ds(at, span), head_cols(h)],
            lambda h: vt_ref[value_rows(h), first:],
            col_ref[BLOCK - halo + first :, :], row_ref[0:1, pl.ds(at, span)], at, out_ref, lse_ref,
        )

    def merge(size):
        first = halo - size
        _, parts, values = project(xm_ref[first:, :], xo_ref[first:, :], wq_ref, wvt_ref)
        store_keys(first, parts, values, key_ref, vt_ref)
        many = 3 * TILE if size == 3 * TILE else TILE
        few = (bits & 255) < 2 ** (many // TILE)

        @pl.when(few & (bits != 0))
        def _():
            at_once(0, first, many)

        @pl.when(jnp.logical_not(few))
        def _():
            @pl.loop(0, BLOCK // TILE)
            def _(i):
                @pl.when(((bits >> i) & 1) != 0)
                def _():
                    at_once(pl.multiple_of(i * TILE, TILE), first, TILE)

    if halo > HALO:
        merge(halo)
    else:
        pl.when(bits < 256)(lambda: merge(TILE))
        pl.when(bits >= 256)(lambda: merge(halo))

    pieces = send_ref.shape[0] // PIECE

    def sending(t):
        piece = pl.ds(pl.multiple_of(t * PIECE, PIECE), PIECE)
        return pltpu.make_async_copy(buf_ref.at[piece], send_ref.at[piece], sem_ref.at[t])

    def complete(piece, codes, rows_ref, cols):
        pick = pick_of(codes, 0, cols.size)
        body = mm_nt(pick, out_ref[:, cols])
        extra = in_meta_row(mm_nt(pick, sums_of(lse_ref[:, cols], heads)))
        rows = jnp.concatenate([body[:, 0:128] + extra, body[:, 128:]], axis=1)
        buf_ref[piece, :] = (rows_ref[piece, :].astype(F32) + rows).astype(BF)

    def finish(span):
        @pl.loop(0, pieces)
        def _(t):
            piece = pl.ds(pl.multiple_of(t * PIECE, PIECE), PIECE)
            complete(piece, place_ref[piece, :], early_ref, pl.ds(0, span))
            sending(t).start()

    needed = bits & 255
    pl.when(needed < 2 ** (SPAN // TILE))(lambda: finish(SPAN))
    pl.when((needed >= 2 ** (SPAN // TILE)) & (needed < 2 ** (2 * SPAN // TILE)))(
        lambda: finish(2 * SPAN)
    )

    @pl.when(needed >= 2 ** (2 * SPAN // TILE))
    def _():
        @pl.loop(0, pieces)
        def _(t):
            piece = pl.ds(pl.multiple_of(t * PIECE, PIECE), PIECE)
            buf_ref[piece, :] = early_ref[piece, :]

            @pl.loop(0, SPANS)
            def _(i):
                @pl.when(late_span(bits, i))
                def _():
                    codes = place_ref[piece, :] - (i * SPAN).astype(F32)
                    cols = pl.ds(pl.multiple_of(i * SPAN, SPAN), SPAN)
                    complete(piece, codes, buf_ref, cols)

            sending(t).start()

    @pl.loop(0, pieces)
    def _(t):
        sending(t).wait()


def final_kernel(x_ref, slot_ref, w_ref, out_ref, buf_ref, sem_ref, *, owners):
    count = out_ref.shape[0]
    width = x_ref.shape[1]
    rows = owners * SLOTS
    lane = iota((count, 128), 1)
    picks, meta_picks, ranks = [], [], []
    for r in range(2):
        slot = slot_ref[r * count : (r + 1) * count, :].astype(I32)
        place = slot & (SLOTS - 1)
        at_meta = slot - place + META
        picks.append(
            jnp.concatenate([mask(slot == lane + c) for c in range(0, rows, 128)], axis=1)
        )
        meta_picks.append(
            jnp.concatenate([mask(at_meta == lane + c) for c in range(0, rows, 128)], axis=1)
        )
        ranks.append(place)
    sums = []
    for r in range(2):
        there = [x_ref[(a * 2 + r) * rows : (a * 2 + r + 1) * rows, 0:128] for a in range(2)]
        own = mm(meta_picks[r], jnp.concatenate(there, axis=1))
        keep = (lane >> 3) == ranks[r]
        sums.append([jnp.where(keep, own[:, a * 128 : (a + 1) * 128], 0.0) for a in range(2)])
    v = iota((256, width), 0)
    select = jnp.where(((v & 7) >> 1) == (iota((256, width), 1) >> 7), 1.0, 0.0)
    select = jnp.where(v < 128, -select, select).astype(BF)
    combined = []
    for a in range(2):
        values = [
            mm(picks[r], x_ref[(a * 2 + r) * rows : (a * 2 + r + 1) * rows, :]) for r in range(2)
        ]
        apart = mm(jnp.concatenate([sums[0][a], sums[1][a]], axis=1).astype(BF), select)
        small = jnp.exp2(-jnp.abs(apart))
        large = 1.0 / (1.0 + small)
        second = jnp.where(apart < 0.0, small * large, large)
        first = jnp.where(apart < 0.0, large, small * large)
        combined.append((first * values[0] + second * values[1]).astype(BF))
    combined = jnp.concatenate(combined, axis=1)
    copies = []
    for part in range(2):
        cols = pl.ds(part * width, width)
        buf_ref[:, cols] = mm(combined, w_ref[:, cols]).astype(BF)
        copies.append(
            pltpu.make_async_copy(buf_ref.at[:, cols], out_ref.at[:, cols], sem_ref.at[part])
        )
        copies[-1].start()
    for copy in copies:
        copy.wait()


def shards(tokens, w_qk, w_v, w_out, positions, buckets):
    tok_dev, model_width = tokens.shape
    owners = lax.axis_size("seq")
    total = 2 * 2 * owners
    width = model_width // 2
    heads = width // DH
    rows = total * SLOTS
    params = pltpu.CompilerParams(vmem_limit_bytes=24 * 2**20)
    alone = pltpu.CompilerParams(vmem_limit_bytes=60 * 2**20)
    in_vmem = pl.BlockSpec(memory_space=pltpu.VMEM)
    in_hbm = pl.BlockSpec(memory_space=pltpu.HBM)

    def shape(*dims, dtype=BF):
        return jax.ShapeDtypeStruct(dims, dtype)

    def cost(flops, moved):
        return pl.CostEstimate(flops=flops, bytes_accessed=moved, transcendentals=0)

    def swap(x):
        return lax.ppermute(x, "round", [(0, 1), (1, 0)])

    def onward(x):
        route = [(chip_of(i), chip_of((i + 1) % owners)) for i in range(owners)]
        return lax.ppermute(x, "seq", route)

    def exchange(x):
        x = x.reshape(total, SLOTS, width)
        x = lax.all_to_all(x, AXES, split_axis=0, concat_axis=0, tiled=True)
        return x.reshape(rows, width)

    packed = pl.pallas_call(
        functools.partial(pack_kernel, owners=owners),
        out_shape=shape(rows, width),
        in_specs=[in_hbm] * 3,
        out_specs=in_hbm,
        scratch_shapes=[
            pltpu.VMEM((tok_dev, model_width), BF),
            pltpu.VMEM(positions.shape, I32),
            pltpu.VMEM(buckets.shape, I32),
            pltpu.VMEM((rows, width), BF),
            pltpu.SemaphoreType.DMA((4,)),
            pltpu.SemaphoreType.DMA((4,)),
        ],
        compiler_params=alone,
        name="pack",
    )(tokens, positions, buckets)
    arrived = exchange(packed)

    wq, wvt, wout, slots = pl.pallas_call(
        functools.partial(prepare_kernel, owners=owners),
        out_shape=[
            shape(model_width, width),
            shape(width, model_width),
            shape(model_width, model_width),
            shape(2 * tok_dev, 128, dtype=F32),
        ],
        in_specs=[in_hbm] * 3 + [in_vmem],
        out_specs=[in_vmem] * 4,
        scratch_shapes=[pltpu.VMEM((model_width, width), BF), pltpu.SemaphoreType.DMA((5,))],
        compiler_params=params,
        cost_estimate=cost(2**30, 8 * 2**20),
        name="prepare",
    )(w_qk, w_v, w_out, positions)
    arrived, wq, wvt, wout, slots = lax.optimization_barrier((arrived, wq, wvt, wout, slots))

    high, meta, codes, wide = pl.pallas_call(
        sort_high_kernel,
        out_shape=[
            shape(HALO, width),
            shape(total, 128),
            shape(total // 8, 128, dtype=F32),
            shape(1, 1, dtype=F32),
        ],
        compiler_params=params,
        name="sort_high",
    )(arrived)
    halo = onward(high)
    high_other = swap(high)
    low, low_next, label_row, label_col, prior_col, flags = pl.pallas_call(
        functools.partial(sort_low_kernel, owners=owners),
        out_shape=[
            shape((BLOCK - HALO) // 2, width),
            shape((BLOCK - HALO) // 2, width),
            shape(1, BLOCK, dtype=F32),
            shape(BLOCK, TILE, dtype=F32),
            shape(BLOCK, TILE, dtype=F32),
            shape(8, 128, dtype=F32),
        ],
        compiler_params=params,
        cost_estimate=cost(4 * BLOCK * rows * width, 4 * 2**20),
        name="sort_low",
    )(arrived, codes)
    low_other, low_next_other = swap(low), swap(low_next)

    values_shape = (heads * (DH + 16), BLOCK)
    q_high, key_high, vt_high, places = pl.pallas_call(
        first_kernel,
        out_shape=[
            shape(HALO, width),
            shape(HALO, 2 * width),
            shape(values_shape[0], HALO),
            shape(rows, 128, dtype=F32),
        ],
        compiler_params=params,
        cost_estimate=cost(4 * HALO * model_width * width, 2**20),
        name="own_rows",
    )(high, high_other, wq, wvt, meta)
    queries, own_out, own_lse, early = pl.pallas_call(
        own_kernel,
        out_shape=[
            shape(BLOCK, width),
            shape(width, BLOCK),
            shape(8, BLOCK, dtype=F32),
            shape(rows, width),
        ],
        scratch_shapes=[pltpu.VMEM((BLOCK, 2 * width), BF), pltpu.VMEM(values_shape, BF)],
        compiler_params=params,
        cost_estimate=cost(2**20, 2**20),
        name="own_block",
    )(
        low, low_next, low_other, low_next_other, q_high, key_high, vt_high, wq, wvt,
        label_row, label_col, flags, places,
    )
    halo, own_lse = lax.optimization_barrier((halo, own_lse))

    def finish(halo_mine, halo_other):
        size = halo_mine.shape[0]
        return pl.pallas_call(
            rest_kernel,
            out_shape=shape(rows, width),
            in_specs=[in_vmem] * 12,
            out_specs=in_hbm,
            scratch_shapes=[
                pltpu.VMEM((width, BLOCK), BF),
                pltpu.VMEM((8, BLOCK), F32),
                pltpu.VMEM((size, 2 * width), BF),
                pltpu.VMEM((heads * (DH + 16), size), BF),
                pltpu.VMEM((rows, width), BF),
                pltpu.SemaphoreType.DMA((rows // PIECE,)),
            ],
            compiler_params=params,
            name="prior_block",
        )(
            halo_mine, halo_other, wq, wvt, label_row, prior_col, flags,
            queries, own_out, own_lse, places, early,
        )

    halo_other = swap(halo)

    def more(rows):
        rest = onward(rows)
        return finish(
            jnp.concatenate([rest, halo], axis=0),
            jnp.concatenate([swap(rest), halo_other], axis=0),
        )

    back = lax.cond(wide[0, 0] > 0.0, lambda: more(jnp.concatenate([low, low_next], axis=0)), lambda: finish(halo, halo_other))
    returned = exchange(back)
    return pl.pallas_call(
        functools.partial(final_kernel, owners=owners),
        out_shape=shape(tok_dev, model_width),
        out_specs=in_hbm,
        scratch_shapes=[
            pltpu.VMEM((tok_dev, model_width), BF),
            pltpu.SemaphoreType.DMA((2,)),
        ],
        compiler_params=params,
        name="combine",
    )(returned, slots, wout)


def solution(mesh):
    in_specs = (
        P(("round", "head", "seq"), None),
        P(),
        P(),
        P(),
        P(None, ("round", "head", "seq")),
        P("round", "seq"),
    )
    out_specs = P(("round", "head", "seq"), None)
    return jax.shard_map(shards, mesh=mesh, in_specs=in_specs, out_specs=out_specs, check_vma=False)
```
